256 devices in a mesh: ctx: 32 (over z_lo, y, x), exp: 8 (over z_hi, core).
Axes of the slice: x: 4, y: 4, z: 8 (z_hi: 4, z_lo: 2; z = z_hi * 2 + z_lo), core: 2. Of those that a mesh axis runs over, the one named last changes fastest.
Arguments:
- tokens: bfloat16 [4096, 2880], P('ctx'), may hold values from -6 to 6
- cotangent: bfloat16 [4096, 2880], P('ctx'), may hold values from -6 to 6
- expert_ids: int32 [4096, 4], P('ctx'), may hold values from 0 to 31, all different within a row; in each aligned block of 128 rows (0 to 127, 128 to 255, ...) at most 20 rows name the same one
- combine_weights: float32 [4096, 4], P('ctx'), may hold values from 0.05 to 1
- w_query: bfloat16 [2880, 2048], P('ctx', 'exp'), may hold values from -0.109375 to 0.109375
- key_value_weight: bfloat16 [2880, 1024], P('ctx', 'exp'), may hold values from -0.109375 to 0.109375
- w_output: bfloat16 [2048, 2880], P('exp', 'ctx'), may hold values from -0.125 to 0.125
- w_gate: bfloat16 [32, 2880, 2048], P('ctx', None, 'exp'), may hold values from -0.109375 to 0.109375
- w_up: bfloat16 [32, 2880, 2048], P('ctx', None, 'exp'), may hold values from -0.109375 to 0.109375
- w_down: bfloat16 [32, 2048, 2880], P('ctx', 'exp'), may hold values from -0.125 to 0.125
Outputs:
- block_out: bfloat16 [4096, 2880], P('ctx')
- grad_tokens: bfloat16 [4096, 2880], P('ctx')
- grad_query: bfloat16 [2880, 2048], P('ctx', 'exp')
- grad_keyval: bfloat16 [2880, 1024], P('ctx', 'exp')
- grad_output: bfloat16 [2048, 2880], P('exp', 'ctx')
- grad_gate: bfloat16 [32, 2880, 2048], P('ctx', None, 'exp')
- grad_up: bfloat16 [32, 2880, 2048], P('ctx', None, 'exp')
- grad_down: bfloat16 [32, 2048, 2880], P('ctx', 'exp')
The draws below stay inside these ranges and needn't reach their ends.
Inputs may be any that keep to these rules, and one draw needn't show every extreme that they name: `expert_ids`: each row names 4 different experts. Within the 128 rows of one context block no expert is named more than 20 times, and in some block one expert is named exactly 20 times.
All inputs are finite; a program needn't handle non-finite values.
Results may differ from the reference program's by a relative error of at most 0.029.
Values may be sent and summed in bfloat16 or wider, within the bound.
A program may use at most 128 MiB of HBM per device.

```python
import math
import jax
import jax.numpy as jnp
import numpy as np
from jax import lax

MODEL_DIM = 2880
QUERY_HEADS = 32
KEY_VALUE_HEADS = 8
HEAD_SIZE = 64
WINDOW = 128
FF = 2048
TOPK = 4
BLOCK_TOKENS = 128
SEQUENCE_TOKENS = 4096
EXPERTS = 32
CAP = 20
N_CTX = 32
N_EXP = 8


def strengthened(values, stream_key, source, target, parts, factor):
    def block_of(axis_at):
        return (jnp.arange(values.shape[axis_at]) // (values.shape[axis_at] // parts)).reshape((-1,) + (1,) * (values.ndim - 1 - axis_at))

    near = jax.random.permutation(stream_key, parts)[block_of(target)]
    second = (block_of(target) + parts // 2) % parts
    return jnp.where((block_of(source) == near) | (block_of(source) == second), factor * values, values)


def shard_levels(key, dims, cuts, least, top_value):
    gain, own = 1.0, jax.random.fold_in(key, 6)
    for axis_at, blocks in cuts:
        draws = jnp.exp(jax.random.uniform(jax.random.fold_in(own, axis_at), (blocks,), jnp.float32, least / len(cuts), top_value / len(cuts)))
        gain = gain * jnp.repeat(draws, dims[axis_at] // blocks).reshape([-1 if axis == axis_at else 1 for axis in range(len(dims))])
    return gain


def assign_block(key, own, number, rows, amount, top, reach, skew):
    sequence = jax.random.permutation(key, amount)
    crowded, ordinary = portions_of(amount, rows * top, reach, skew, True), portions_of(amount, rows * top, reach, skew, False)
    places = jnp.arange(amount)

    def named(lengths, turn):
        used = int((lengths > 0).sum())
        fixed = max(1, used // 4)
        shifted = fixed + (places - fixed + turn * (used - fixed)) % max(1, amount - fixed)
        return jnp.zeros((amount,), jnp.int32).at[sequence[jnp.where(places < fixed, places, shifted)]].set(jnp.asarray(lengths, jnp.int32))

    lengths = jnp.where(number % 4 == 0, named(crowded, number // 4), named(ordinary, number - number // 4 - 1))
    mixed = jax.random.permutation(jax.random.fold_in(own, 3), amount)
    donor, sink = mixed[0:amount // 2 * 2:2], mixed[1:amount // 2 * 2:2]
    margin = jnp.minimum(lengths[donor] - 1, reach - lengths[sink]) // 2
    margin = jnp.where((donor == sequence[0]) | (sink == sequence[0]) | (lengths[sink] == 0), 0, jnp.maximum(margin, 0))
    shifted = jax.random.randint(jax.random.fold_in(own, 4), (amount // 2,), 0, 1 << 20) % (margin + 1)
    lengths = lengths.at[donor].add(-shifted).at[sink].add(shifted)
    labels = jnp.searchsorted(jnp.cumsum(lengths), jnp.arange(rows * top), side="right").astype(jnp.int32)
    listing = labels.reshape(top, rows).T
    listing = listing[jax.random.permutation(jax.random.fold_in(own, 1), rows)]
    turn = jax.random.randint(jax.random.fold_in(own, 2), (rows, 1), 0, top)
    return jnp.take_along_axis(listing, (jnp.arange(top)[None, :] + turn) % top, axis=1)


def portions_of(number_of, total, reach, slope, full):
    weights = [(1 << 20) // math.isqrt(grade ** slope) + 1 for grade in range(1, number_of + 1)]
    largest = reach if full else min(reach, max(-(-total // number_of), total * weights[0] // sum(weights)))
    least = 1 if total - largest >= number_of - 1 else 0
    given, spare = [largest] + [least] * (number_of - 1), total - largest - least * (number_of - 1)
    while spare > 0:
        candidates = [i for i in range(1, number_of) if given[i] < largest] or [i for i in range(1, number_of) if given[i] < reach]
        pool, remaining = sum([weights[i] for i in candidates]), spare
        for i in candidates:
            more = min(reach - given[i], max(1, remaining * weights[i] // pool), spare)
            given[i] = given[i] + more
            spare = spare - more
    return np.array(given)


def scatter_about(stream_key, dims, spread, reach, split=(), kind=jnp.bfloat16):
    drawn = jax.random.normal(stream_key, dims, jnp.float32) * spread
    if len(split) > 0:
        drawn = shard_levels(stream_key, dims, split, -0.22, 0.18) * drawn
    return jnp.clip(drawn, min=-reach, max=reach).astype(kind)


def noise_with(own_key, shape, spread, bound, shards, heavy, held_as=jnp.bfloat16):
    array = spread * jax.random.normal(own_key, shape, jnp.float32)
    if shards:
        array = array * shard_levels(own_key, shape, shards, -0.22, 0.18)
    return jnp.clip(strengthened(array, jax.random.fold_in(own_key, 3), *heavy), -bound, bound).astype(held_as)


def setup_inputs(seed: int = 0) -> dict:
    splits = jax.random.split(jax.random.key(seed), 11)
    tokens = scatter_about(splits[0], (SEQUENCE_TOKENS, MODEL_DIM), 1.0, 6.0, ((0, 32),))
    cotangent = noise_with(splits[1], (SEQUENCE_TOKENS, MODEL_DIM), 1.0, 6.0, ((0, 32),), (0, 1, 32, 2.75))
    expert_ids_keys = jax.random.split(jax.random.fold_in(splits[2], 1), SEQUENCE_TOKENS // BLOCK_TOKENS)
    expert_ids_turns = jax.random.permutation(jax.random.fold_in(splits[2], 3), SEQUENCE_TOKENS // BLOCK_TOKENS)
    expert_ids = jax.vmap(lambda own, number: assign_block(jax.random.fold_in(splits[2], 2), own, number, BLOCK_TOKENS, EXPERTS, TOPK, CAP, 2))(expert_ids_keys, expert_ids_turns).reshape((SEQUENCE_TOKENS, TOPK))
    combine_weights = jnp.clip(jnp.exp(math.log(1.0) - 2.9957323 * jax.random.uniform(splits[3], (SEQUENCE_TOKENS, TOPK), jnp.float32) ** shard_levels(splits[3], (SEQUENCE_TOKENS, TOPK), ((0, 32),), -0.2, 0.2)), 0.05, 1.0)
    w_query = scatter_about(splits[4], (MODEL_DIM, QUERY_HEADS * HEAD_SIZE), MODEL_DIM ** -0.5, 0.109375, ((0, 32), (1, 8)))
    key_value_weight = scatter_about(splits[5], (MODEL_DIM, 2 * KEY_VALUE_HEADS * HEAD_SIZE), MODEL_DIM ** -0.5, 0.109375, ((0, 32), (1, 8)))
    w_output = scatter_about(splits[6], (QUERY_HEADS * HEAD_SIZE, MODEL_DIM), (QUERY_HEADS * HEAD_SIZE) ** -0.5, 0.125, ((0, 8), (1, 32)))
    w_gate = scatter_about(splits[7], (EXPERTS, MODEL_DIM, FF), MODEL_DIM ** -0.5, 0.109375, ((0, 32), (2, 8)))
    w_up = scatter_about(splits[8], (EXPERTS, MODEL_DIM, FF), MODEL_DIM ** -0.5, 0.109375, ((0, 32), (2, 8)))
    w_down = scatter_about(splits[9], (EXPERTS, FF, MODEL_DIM), FF ** -0.5, 0.125, ((0, 32), (1, 8)))
    return {"tokens": tokens, "cotangent": cotangent, "expert_ids": expert_ids, "combine_weights": combine_weights, "w_query": w_query, "key_value_weight": key_value_weight, "w_output": w_output, "w_gate": w_gate, "w_up": w_up, "w_down": w_down}


EPSILON = 1e-05
GLU_ALPHA = 1.702

def rms_norm(values):
    inv_rms = lax.rsqrt(lax.optimization_barrier(jnp.mean(values * values, axis=-1, keepdims=True)) + EPSILON)
    return (values * inv_rms, inv_rms)

def rms_back(values, inv_rms, grad_in):
    inner_mean = lax.optimization_barrier(jnp.mean(grad_in * values, axis=-1, keepdims=True))
    return inv_rms * grad_in - values * (inv_rms * inv_rms * inv_rms) * inner_mean

def rounded(values):
    return lax.optimization_barrier(values.astype(jnp.bfloat16)).astype(jnp.float32)

def band_valid(row_count, band_width, block_idx):
    query_pos = block_idx * row_count + jnp.arange(row_count)[:, None]
    key_pos = block_idx * row_count - band_width + jnp.arange(band_width + row_count)[None, :]
    return (key_pos <= query_pos) & (key_pos > query_pos - band_width) & (key_pos >= 0)

def attend(query_matrix, key_value, valid_mask):
    query_f = query_matrix.astype(jnp.float32)
    key_rows = key_value[:, :, 0].astype(jnp.float32)
    value_rows = key_value[:, :, 1].astype(jnp.float32)
    scores = jnp.einsum('tgjd,sgd->gjts', query_f, key_rows) * 0.125
    weights = jnp.where(valid_mask, jnp.exp(scores), 0.0)
    probability_single = weights / lax.optimization_barrier(jnp.sum(weights, axis=-1, keepdims=True))
    probability_half = probability_single.astype(jnp.bfloat16)
    attended = jnp.einsum('gjts,sgd->tgjd', probability_half.astype(jnp.float32), value_rows)
    return (attended.astype(jnp.bfloat16), probability_single, probability_half)

def attention_backward(query_matrix, key_value, probability_single, probability_half, grad_out):
    query_f = query_matrix.astype(jnp.float32)
    key_rows = key_value[:, :, 0].astype(jnp.float32)
    value_rows = key_value[:, :, 1].astype(jnp.float32)
    grad_f = grad_out.astype(jnp.float32)
    grad_prob = jnp.einsum('tgjd,sgd->gjts', grad_f, value_rows)
    grad_value = jnp.einsum('gjts,tgjd->sgd', probability_half.astype(jnp.float32), grad_f)
    grad_score = (probability_single * (grad_prob - lax.optimization_barrier(jnp.sum(grad_prob * probability_single, axis=-1, keepdims=True))) * 0.125).astype(jnp.bfloat16)
    score_f = grad_score.astype(jnp.float32)
    query_gradients = jnp.einsum('gjts,sgd->tgjd', score_f, key_rows)
    grad_key = jnp.einsum('gjts,tgjd->sgd', score_f, query_f)
    return (query_gradients, jnp.stack([grad_key, grad_value], axis=2))

def place_routes(flat_ids, expert_count, capacity):
    one_hot = (flat_ids[:, None] == jnp.arange(expert_count)[None, :]).astype(jnp.int32)
    earlier = jnp.cumsum(one_hot, axis=0) - one_hot
    return (flat_ids * capacity + lax.optimization_barrier(jnp.sum(earlier * one_hot, axis=1))).astype(jnp.int32)

def reference(tokens, cotangent, expert_ids, combine_weights, w_query, key_value_weight, w_output, w_gate, w_up, w_down):
    query_head_group = QUERY_HEADS // KEY_VALUE_HEADS
    group_units = FF // N_EXP
    tokens_f32 = tokens.astype(jnp.float32)
    normed_f32, token_scale = rms_norm(tokens_f32)
    normed = normed_f32.astype(jnp.bfloat16)
    query_matrix = jnp.dot(normed, w_query, preferred_element_type=jnp.float32).astype(jnp.bfloat16)
    key_value = jnp.dot(normed, key_value_weight, preferred_element_type=jnp.float32).astype(jnp.bfloat16)
    query_block_list = query_matrix.reshape(N_CTX, BLOCK_TOKENS, KEY_VALUE_HEADS, query_head_group, HEAD_SIZE)
    key_value_blocks = key_value.reshape(N_CTX, BLOCK_TOKENS, KEY_VALUE_HEADS, 2, HEAD_SIZE)
    prev_rims = jnp.concatenate([jnp.zeros_like(key_value_blocks[:1, BLOCK_TOKENS - WINDOW:]), key_value_blocks[:-1, BLOCK_TOKENS - WINDOW:]], axis=0)
    banded_key_span = jnp.concatenate([prev_rims, key_value_blocks], axis=1)
    valid_mask = jax.vmap(lambda block_idx: band_valid(BLOCK_TOKENS, WINDOW, block_idx))(jnp.arange(N_CTX))
    attended, probability_single, probability_half = jax.vmap(attend)(query_block_list, banded_key_span, valid_mask)
    attended_flat = attended.reshape(SEQUENCE_TOKENS, QUERY_HEADS * HEAD_SIZE)
    residual = (tokens_f32 + jnp.dot(attended_flat, w_output, preferred_element_type=jnp.float32)).astype(jnp.bfloat16)
    residual_f32 = residual.astype(jnp.float32)
    moe_f32, resid_scale = rms_norm(residual_f32)
    moe_input = moe_f32.astype(jnp.bfloat16)
    target = jax.vmap(lambda ids_block: place_routes(ids_block, EXPERTS, CAP))(expert_ids.reshape(N_CTX, BLOCK_TOKENS * TOPK))

    def scatter_rows(slot_index, row_values):
        return jnp.zeros((EXPERTS * CAP, MODEL_DIM), jnp.bfloat16).at[slot_index].set(row_values)

    def to_experts(sent_rows):
        return sent_rows.reshape(N_CTX, EXPERTS, CAP, MODEL_DIM).transpose(1, 0, 2, 3).reshape(EXPERTS, N_CTX * CAP, MODEL_DIM)

    def to_sources(expert_rows):
        return expert_rows.reshape(EXPERTS, N_CTX, CAP, MODEL_DIM).transpose(1, 0, 2, 3).reshape(N_CTX, EXPERTS * CAP, MODEL_DIM)
    moe_rows = jnp.repeat(moe_input.reshape(N_CTX, BLOCK_TOKENS, MODEL_DIM), TOPK, axis=1)
    incoming = to_experts(jax.vmap(scatter_rows)(target, moe_rows))
    route_scale = combine_weights.reshape(N_CTX, BLOCK_TOKENS, TOPK, 1)
    cot_f32 = cotangent.astype(jnp.float32)
    grad_rows = (route_scale * cot_f32.reshape(N_CTX, BLOCK_TOKENS, 1, MODEL_DIM)).astype(jnp.bfloat16).reshape(N_CTX, BLOCK_TOKENS * TOPK, MODEL_DIM)
    grad_incoming = to_experts(jax.vmap(scatter_rows)(target, grad_rows))

    def expert_step(operands):
        expert_rows, grad_expert, gate_w, up_w, down_w = operands
        gate_pre = jnp.dot(expert_rows, gate_w, preferred_element_type=jnp.float32)
        up_pre = jnp.dot(expert_rows, up_w, preferred_element_type=jnp.float32)
        gate_sig = jax.nn.sigmoid(GLU_ALPHA * gate_pre)
        gate_glu = gate_pre * gate_sig
        activated = (gate_glu * (up_pre + 1.0)).astype(jnp.bfloat16)
        down_groups = jnp.einsum('rgf,gfd->grd', activated.reshape(-1, N_EXP, group_units).astype(jnp.float32), down_w.reshape(N_EXP, group_units, MODEL_DIM).astype(jnp.float32))
        expert_out = lax.optimization_barrier(jnp.sum(rounded(down_groups), axis=0))
        grad_act = jnp.dot(grad_expert, down_w.T, preferred_element_type=jnp.float32)
        grad_gate_pre = (grad_act * (up_pre + 1.0) * (gate_sig + GLU_ALPHA * gate_glu * (1.0 - gate_sig))).astype(jnp.bfloat16)
        grad_up_pre = (grad_act * gate_glu).astype(jnp.bfloat16)
        grad_down_e = jnp.dot(activated.T, grad_expert, preferred_element_type=jnp.float32).astype(jnp.bfloat16)
        grad_gate_e = jnp.dot(expert_rows.T, grad_gate_pre, preferred_element_type=jnp.float32).astype(jnp.bfloat16)
        grad_up_e = jnp.dot(expert_rows.T, grad_up_pre, preferred_element_type=jnp.float32).astype(jnp.bfloat16)
        input_groups = jnp.einsum('rgf,gfd->grd', grad_gate_pre.reshape(-1, N_EXP, group_units).astype(jnp.float32), gate_w.T.reshape(N_EXP, group_units, MODEL_DIM).astype(jnp.float32))
        input_groups = input_groups + jnp.einsum('rgf,gfd->grd', grad_up_pre.reshape(-1, N_EXP, group_units).astype(jnp.float32), up_w.T.reshape(N_EXP, group_units, MODEL_DIM).astype(jnp.float32))
        expert_back = lax.optimization_barrier(jnp.sum(rounded(input_groups), axis=0))
        return (expert_out, expert_back, grad_gate_e, grad_up_e, grad_down_e)
    expert_outs, expert_backs, grad_gate, grad_up, grad_down = lax.map(expert_step, (incoming, grad_incoming, w_gate, w_up, w_down))
    out_tables = to_sources(expert_outs)
    back_tables = to_sources(expert_backs)

    def weighted_rows(table, slot_index, weights):
        picked = table[slot_index].reshape(BLOCK_TOKENS, TOPK, MODEL_DIM)
        return lax.optimization_barrier(jnp.sum(picked * weights[:, :, None], axis=1))

    def plain_rows(table, slot_index):
        return lax.optimization_barrier(jnp.sum(table[slot_index].reshape(BLOCK_TOKENS, TOPK, MODEL_DIM), axis=1))
    moe_total = jax.vmap(weighted_rows)(out_tables, target, combine_weights.reshape(N_CTX, BLOCK_TOKENS, TOPK)).reshape(SEQUENCE_TOKENS, MODEL_DIM)
    block_out = (residual_f32 + moe_total).astype(jnp.bfloat16)
    grad_normed = jax.vmap(plain_rows)(back_tables, target).reshape(SEQUENCE_TOKENS, MODEL_DIM)
    grad_resid = cot_f32 + rms_back(residual_f32, resid_scale, grad_normed)
    grad_resid_bf = grad_resid.astype(jnp.bfloat16)
    attended_gradient = jnp.dot(grad_resid_bf, w_output.T, preferred_element_type=jnp.float32).astype(jnp.bfloat16)
    query_gradients, key_value_gradients = jax.vmap(attention_backward)(query_block_list, banded_key_span, probability_single, probability_half, attended_gradient.reshape(N_CTX, BLOCK_TOKENS, KEY_VALUE_HEADS, query_head_group, HEAD_SIZE))
    rim_grads = key_value_gradients[:, :WINDOW]
    carried = jnp.concatenate([rim_grads[1:], jnp.zeros_like(rim_grads[:1])], axis=0)
    local_gradient = key_value_gradients[:, WINDOW:].at[:, BLOCK_TOKENS - WINDOW:].add(carried)
    key_value_grad = local_gradient.reshape(SEQUENCE_TOKENS, 2 * KEY_VALUE_HEADS * HEAD_SIZE).astype(jnp.bfloat16)
    query_grad = query_gradients.reshape(SEQUENCE_TOKENS, QUERY_HEADS * HEAD_SIZE).astype(jnp.bfloat16)
    grad_normed_in = jnp.dot(query_grad, w_query.T, preferred_element_type=jnp.float32) + jnp.dot(key_value_grad, key_value_weight.T, preferred_element_type=jnp.float32)
    grad_tokens = (grad_resid + rms_back(tokens_f32, token_scale, grad_normed_in)).astype(jnp.bfloat16)

    def block_sum(left, right):
        left_blocks = left.reshape(N_CTX, BLOCK_TOKENS, left.shape[1])
        right_blocks = right.reshape(N_CTX, BLOCK_TOKENS, right.shape[1])

        def add_block(total, pair):
            return (total + rounded(jnp.dot(pair[0].T, pair[1], preferred_element_type=jnp.float32)), None)
        total, _ = lax.scan(add_block, jnp.zeros((left.shape[1], right.shape[1]), jnp.float32), (left_blocks, right_blocks))
        return total.astype(jnp.bfloat16)
    grad_query = block_sum(normed, query_grad)
    grad_keyval = block_sum(normed, key_value_grad)
    grad_output = block_sum(attended_flat, grad_resid_bf)
    return (block_out, grad_tokens, grad_query, grad_keyval, grad_output, grad_gate, grad_up, grad_down)
```

```python
import functools

import jax
import jax.numpy as jnp
from jax import lax
from jax.experimental import pallas as pl
from jax.experimental.pallas import tpu as pltpu
from jax.sharding import PartitionSpec as P

CTX, EXP = "ctx", "exp"
SHARD = 90
PADDED = 96
HALF_LANES = 1920
MESH = pl.DeviceIdType.MESH
VMEM_BYTES = 60 * 2**20


def params(collective_id):
    return pltpu.CompilerParams(
        collective_id=collective_id, has_side_effects=True, vmem_limit_bytes=VMEM_BYTES
    )


def vmem_specs(count):
    return [pl.BlockSpec(memory_space=pltpu.VMEM)] * count


def place():
    c = lax.axis_index(CTX)
    return c, c // 16, (c // 4) % 4, c % 4


def greet(peers):
    barrier = pltpu.get_barrier_semaphore()
    for peer in peers:
        pl.semaphore_signal(barrier, inc=1, device_id=peer, device_id_type=MESH)
    pl.semaphore_wait(barrier, len(peers))


def gather_kernel(w_ref, out_ref, send, recv):
    c, z, y, x = place()
    e = lax.axis_index(EXP)

    def dev(zz, yy, xx):
        return (zz * 16 + ((yy + 4) % 4) * 4 + (xx + 4) % 4, e)

    def copy(n, src, dst, to):
        cp = pltpu.make_async_remote_copy(
            src_ref=src, dst_ref=dst, send_sem=send.at[n], recv_sem=recv.at[n],
            device_id=to, device_id_type=MESH,
        )
        cp.start()
        return cp

    greet([dev(1 - z, y, x), dev(z, y + 1, x), dev(z, y - 1, x), dev(z, y, x + 1), dev(z, y, x - 1)])
    rows = (pl.ds(0, 48), pl.ds(48, 48))
    copies = []
    first = []
    for h in range(2):
        first.append(copy(h, w_ref.at[rows[h]], out_ref.at[z, y, x, rows[h]], dev(1 - z, y, x)))
    out_ref[z, y, x] = w_ref[...]
    copies += first

    def view(h, phase, zsel, pos):
        along_x = (h == 0) == (phase == 1)
        if phase == 1:
            return out_ref.at[zsel, y, pos, rows[h]] if along_x else out_ref.at[zsel, pos, x, rows[h]]
        return out_ref.at[zsel, :, pos, rows[h]] if along_x else out_ref.at[zsel, pos, :, rows[h]]

    def ring(h, phase):
        along_x = (h == 0) == (phase == 1)
        me = x if along_x else y
        up = dev(z, y, x + 1) if along_x else dev(z, y + 1, x)
        down = dev(z, y, x - 1) if along_x else dev(z, y - 1, x)
        return me, (me + 3) % 4, (me + 1) % 4, up, down

    for phase in (1, 2):
        direct = []
        for h in range(2):
            for cp in first[h] if phase == 2 else (first[h],):
                cp.wait_recv()
            me, low, high, up, down = ring(h, phase)
            n = 2 + (phase - 1) * 8 + h * 4
            both = pl.ds(0, 2)
            direct.append((
                copy(n, view(h, phase, both, me), view(h, phase, both, me), up),
                copy(n + 1, view(h, phase, both, me), view(h, phase, both, me), down),
            ))
        later = []
        for h in range(2):
            me, low, high, up, down = ring(h, phase)
            n = 2 + (phase - 1) * 8 + h * 4
            direct[h][0].wait_recv()
            a = copy(n + 2, view(h, phase, 0, low), view(h, phase, 0, low), up)
            direct[h][1].wait_recv()
            b = copy(n + 3, view(h, phase, 1, high), view(h, phase, 1, high), down)
            later.append((a, b))
        for h in range(2):
            copies += [*direct[h], *later[h]]
        first = later
    for h in range(2):
        for cp in first[h]:
            cp.wait_recv()
    for cp in copies:
        cp.wait_send()


def gather_weights(shard):
    out = pl.pallas_call(
        gather_kernel,
        out_shape=jax.ShapeDtypeStruct((2, 4, 4, PADDED, 640), jnp.bfloat16),
        in_specs=vmem_specs(1),
        out_specs=vmem_specs(1)[0],
        scratch_shapes=[pltpu.SemaphoreType.DMA((18,)), pltpu.SemaphoreType.DMA((18,))],
        compiler_params=params(0),
        name="gather_weights",
    )(shard)
    return out.reshape(32 * PADDED, 640)


def f32(v):
    return v.astype(jnp.float32)


def bf(v):
    return v.astype(jnp.bfloat16)


def scatter_kernel(t_ref, out_ref, far, near, stage, acc1, far2, near2, stage2, acc2, last, send, recv):
    c, z, y, x = place()
    e = lax.axis_index(EXP)

    def dev(zz, yy, xx):
        return (zz * 16 + ((yy + 4) % 4) * 4 + (xx + 4) % 4, e)

    def copy(n, src, dst, to):
        cp = pltpu.make_async_remote_copy(
            src_ref=src, dst_ref=dst, send_sem=send.at[n], recv_sem=recv.at[n],
            device_id=to, device_id_type=MESH,
        )
        cp.start()
        return cp

    greet([dev(1 - z, y, x), dev(z, y + 1, x), dev(z, y - 1, x), dev(z, y, x + 1), dev(z, y, x - 1)])
    rows = (pl.ds(0, 48), pl.ds(48, 48))
    copies = []

    def ring(along_x):
        me = x if along_x else y
        up = dev(z, y, x + 1) if along_x else dev(z, y + 1, x)
        down = dev(z, y, x - 1) if along_x else dev(z, y - 1, x)
        return me, (me + 3) % 4, (me + 1) % 4, (me + 2) % 4, up, down

    def step(phase, source, far_ref, near_ref, stage_ref):
        started = []
        for h in range(2):
            me, low, high, across, up, down = ring((h == 1) == (phase == 1))
            n = (phase - 1) * 12 + h * 6
            started.append([
                copy(n, source(h, 0, across), far_ref.at[h, 0], up),
                copy(n + 1, source(h, 1, across), far_ref.at[h, 1], down),
                copy(n + 2, source(h, 1, high), near_ref.at[h, 0, 1], up),
                copy(n + 3, source(h, 0, low), near_ref.at[h, 1, 0], down),
            ])
        for h in range(2):
            me, low, high, across, up, down = ring((h == 1) == (phase == 1))
            n = (phase - 1) * 12 + h * 6
            started[h][0].wait_recv()
            stage_ref[h, 0] = bf(f32(source(h, 0, high)[...]) + f32(far_ref[h, 0]))
            started[h].append(copy(n + 4, stage_ref.at[h, 0], near_ref.at[h, 0, 0], up))
            started[h][1].wait_recv()
            stage_ref[h, 1] = bf(f32(source(h, 1, low)[...]) + f32(far_ref[h, 1]))
            started[h].append(copy(n + 5, stage_ref.at[h, 1], near_ref.at[h, 1, 1], down))
        return started

    def first_source(h, zsel, pos):
        return t_ref.at[zsel, pos, :, rows[h]] if h == 0 else t_ref.at[zsel, :, pos, rows[h]]

    started = step(1, first_source, far, near, stage)
    for h in range(2):
        me = ring(h == 1)[0]
        for i in (2, 3, 4, 5):
            started[h][i].wait_recv()
        for zz in range(2):
            acc1[h, zz] = bf(f32(first_source(h, zz, me)[...]) + f32(near[h, 0, zz]) + f32(near[h, 1, zz]))
        copies += started[h]

    def second_source(h, zsel, pos):
        return acc1.at[h, zsel, pos]

    started = step(2, second_source, far2, near2, stage2)
    final = []
    for h in range(2):
        me = ring(h == 0)[0]
        for i in (2, 3, 4, 5):
            started[h][i].wait_recv()
        for zz in range(2):
            acc2[h, zz] = bf(f32(second_source(h, zz, me)[...]) + f32(near2[h, 0, zz]) + f32(near2[h, 1, zz]))
        copies += started[h]
        final.append(copy(24 + h, acc2.at[h, 1 - z], last.at[h], dev(1 - z, y, x)))
    for h in range(2):
        final[h].wait_recv()
        out_ref[rows[h], :] = bf(f32(acc2[h, z]) + f32(last[h]))
    for cp in copies + final:
        cp.wait_send()


def scatter_sums(terms):
    b = jnp.bfloat16
    return pl.pallas_call(
        scatter_kernel,
        out_shape=jax.ShapeDtypeStruct((PADDED, 640), b),
        in_specs=vmem_specs(1),
        out_specs=vmem_specs(1)[0],
        scratch_shapes=[
            pltpu.VMEM((2, 2, 4, 48, 640), b),
            pltpu.VMEM((2, 2, 2, 4, 48, 640), b),
            pltpu.VMEM((2, 2, 4, 48, 640), b),
            pltpu.VMEM((2, 2, 4, 48, 640), b),
            pltpu.VMEM((2, 2, 48, 640), b),
            pltpu.VMEM((2, 2, 2, 48, 640), b),
            pltpu.VMEM((2, 2, 48, 640), b),
            pltpu.VMEM((2, 2, 48, 640), b),
            pltpu.VMEM((2, 48, 640), b),
            pltpu.SemaphoreType.DMA((26,)),
            pltpu.SemaphoreType.DMA((26,)),
        ],
        compiler_params=params(1),
        name="scatter_sums",
    )(terms.reshape(2, 4, 4, PADDED, 640))


def shifted_by(z, y, x, i, sign):
    dz, dy, dx = i // 16, (i // 4) % 4, i % 4
    return ((z + dz) % 2) * 16 + ((y + sign * dy + 4) % 4) * 4 + (x + sign * dx + 4) % 4


def greet_all(c, z, y, x, e, partner):
    barrier = pltpu.get_barrier_semaphore()

    def hello(i, carry):
        pl.semaphore_signal(
            barrier, inc=1, device_id=(shifted_by(z, y, x, i, 1), e), device_id_type=MESH
        )
        return carry

    lax.fori_loop(1, 32, hello, 0)
    pl.semaphore_signal(barrier, inc=1, device_id=partner, device_id_type=MESH)
    pl.semaphore_wait(barrier, 32)


def dispatch_kernel(arrays, *refs):
    ins, outs = refs[:arrays], refs[arrays : 2 * arrays]
    send, recv, send2, recv2 = refs[2 * arrays :]
    c, z, y, x = place()
    e = lax.axis_index(EXP)
    k = e % 2
    partner = (c, e + 1 - 2 * k)
    greet_all(c, z, y, x, e, partner)
    for a in range(arrays):
        outs[a][k, c] = ins[a][k, c]

    def out_copy(a, i):
        to = shifted_by(z, y, x, i, 1)
        return pltpu.make_async_remote_copy(
            src_ref=ins[a].at[k, to], dst_ref=outs[a].at[k, c],
            send_sem=send.at[a, i], recv_sem=recv.at[a, i],
            device_id=(to, e), device_id_type=MESH,
        )

    def across(a, i):
        source = shifted_by(z, y, x, i, -1)
        return pltpu.make_async_remote_copy(
            src_ref=outs[a].at[k, source], dst_ref=outs[a].at[k, source],
            send_sem=send2.at[a, i], recv_sem=recv2.at[a, i],
            device_id=partner, device_id_type=MESH,
        )

    for a in range(arrays):
        lax.fori_loop(1, 32, lambda i, t, a=a: (out_copy(a, i).start(), t)[1], 0)
    for a in range(arrays):
        across(a, 0).start()

    def arrived(a, i, t):
        out_copy(a, i).wait_recv()
        across(a, i).start()
        return t

    for a in range(arrays):
        lax.fori_loop(1, 32, lambda i, t, a=a: arrived(a, i, t), 0)

    def ended(a, i, t):
        across(a, i).wait()
        return t

    for a in range(arrays):
        lax.fori_loop(0, 32, lambda i, t, a=a: ended(a, i, t), 0)
        lax.fori_loop(1, 32, lambda i, t, a=a: (out_copy(a, i).wait_send(), t)[1], 0)


def dispatch(*packed):
    count = len(packed)
    shape = jax.ShapeDtypeStruct((2, 32, 16, HALF_LANES), jnp.bfloat16)
    return pl.pallas_call(
        functools.partial(dispatch_kernel, count),
        out_shape=[shape] * count,
        in_specs=vmem_specs(count),
        out_specs=vmem_specs(count),
        scratch_shapes=[pltpu.SemaphoreType.DMA((count, 32))] * 4,
        compiler_params=params(2),
        name="dispatch_rows",
    )(*packed)


def giveback_kernel(arrays, *refs):
    ins, outs = refs[:arrays], refs[arrays : 2 * arrays]
    other, stage, send, recv, send2, recv2 = refs[2 * arrays :]
    c, z, y, x = place()
    e = lax.axis_index(EXP)
    k = e % 2
    partner = (c, e + 1 - 2 * k)
    greet_all(c, z, y, x, e, partner)

    def across(a, i):
        to = shifted_by(z, y, x, i, 1)
        return pltpu.make_async_remote_copy(
            src_ref=ins[a].at[1 - k, to], dst_ref=other.at[a, to],
            send_sem=send2.at[a, i], recv_sem=recv2.at[a, i],
            device_id=partner, device_id_type=MESH,
        )

    def home(a, i):
        to = shifted_by(z, y, x, i, 1)
        return pltpu.make_async_remote_copy(
            src_ref=stage.at[a, to], dst_ref=outs[a].at[c],
            send_sem=send.at[a, i], recv_sem=recv.at[a, i],
            device_id=(to, e), device_id_type=MESH,
        )

    for a in range(arrays):
        lax.fori_loop(1, 32, lambda i, t, a=a: (across(a, i).start(), t)[1], 0)
        across(a, 0).start()

    def added(a, i, t):
        across(a, i).wait_recv()
        to = shifted_by(z, y, x, i, 1)
        stage[a, to] = bf(f32(ins[a][k, to]) + f32(other[a, to]))
        home(a, i).start()
        return t

    for a in range(arrays):
        lax.fori_loop(1, 32, lambda i, t, a=a: added(a, i, t), 0)
        across(a, 0).wait_recv()
        outs[a][c] = bf(f32(ins[a][k, c]) + f32(other[a, c]))
    for a in range(arrays):
        lax.fori_loop(1, 32, lambda i, t, a=a: (home(a, i).wait(), t)[1], 0)
        lax.fori_loop(0, 32, lambda i, t, a=a: (across(a, i).wait_send(), t)[1], 0)


def giveback(*parts):
    count = len(parts)
    b = jnp.bfloat16
    return pl.pallas_call(
        functools.partial(giveback_kernel, count),
        out_shape=[jax.ShapeDtypeStruct((32, 16, HALF_LANES), b)] * count,
        in_specs=vmem_specs(count),
        out_specs=vmem_specs(count),
        scratch_shapes=[
            pltpu.VMEM((count, 32, 16, HALF_LANES), b),
            pltpu.VMEM((count, 32, 16, HALF_LANES), b),
        ] + [pltpu.SemaphoreType.DMA((count, 32))] * 4,
        compiler_params=params(3),
        name="return_rows",
    )(*parts)


def sum_kernel(post, extra_in, extra_out, *refs):
    part = refs[0]
    ins = refs[1 : 1 + extra_in]
    out = refs[1 + extra_in]
    outs = refs[2 + extra_in : 2 + extra_in + extra_out]
    mate, stage, got, send, recv = refs[2 + extra_in + extra_out :]
    c = lax.axis_index(CTX)
    e = lax.axis_index(EXP)
    h, k = e // 2, e % 2
    partner = (c, e + 1 - 2 * k)

    def peer(d):
        return (c, ((h + d) % 4) * 2 + k)

    greet([partner, peer(1), peer(2), peer(3)])

    def rows(core, block):
        return pl.ds(pl.multiple_of(core * 64 + block * 16, 16), 16)

    def copy(n, src, dst, to):
        cp = pltpu.make_async_remote_copy(
            src_ref=src, dst_ref=dst, send_sem=send.at[n], recv_sem=recv.at[n],
            device_id=to, device_id_type=MESH,
        )
        cp.start()
        return cp

    order = (2, 1, 3, 0)
    copies, pair, far = [], {}, {}
    for d in order:
        b = (h + d) % 4
        pair[d] = copy(d, part.at[rows(1 - k, b)], mate.at[b], partner)
    for d in order:
        b = (h + d) % 4
        pair[d].wait_recv()
        both = f32(part[rows(k, b), :]) + f32(mate[b])
        if d:
            stage[d - 1] = bf(both)
            far[d] = copy(4 + d, stage.at[d - 1], got.at[d - 1], peer(d))
    total = both
    for d in (1, 3, 2):
        far[d].wait_recv()
        total = total + f32(got[d - 1])
    mine = rows(k, h)
    out[mine, :] = post(total, mine, *ins, *outs)
    spread = {d: copy(8 + d, out.at[mine], out.at[mine], peer(d)) for d in (2, 1, 3)}
    passed = [copy(12, out.at[mine], out.at[mine], partner)]
    for d in (1, 3, 2):
        spread[d].wait_recv()
        theirs = rows(k, (h - d + 4) % 4)
        passed.append(copy(12 + d, out.at[theirs], out.at[theirs], partner))
    for cp in passed:
        cp.wait_recv()
    for cp in [*pair.values(), *far.values(), *spread.values(), *passed]:
        cp.wait_send()


def sum_heads(part, post, ins, collective_id, extra_outs=(), name="sum_heads"):
    b = jnp.bfloat16
    width = part.shape[1]
    res = pl.pallas_call(
        functools.partial(sum_kernel, post, len(ins), len(extra_outs)),
        out_shape=[jax.ShapeDtypeStruct((128, width), b), *extra_outs],
        in_specs=vmem_specs(1 + len(ins)),
        out_specs=vmem_specs(1 + len(extra_outs)),
        scratch_shapes=[
            pltpu.VMEM((4, 16, width), b),
            pltpu.VMEM((3, 16, width), b),
            pltpu.VMEM((3, 16, width), b),
            pltpu.SemaphoreType.DMA((16,)),
            pltpu.SemaphoreType.DMA((16,)),
        ],
        compiler_params=params(collective_id),
        name=name,
    )(part, *ins)
    return res


EPSILON = 1e-05
GLU_ALPHA = 1.702
QUERY_HEADS = 32
KEY_VALUE_HEADS = 8
HEAD_SIZE = 64
WINDOW = 128
MODEL = 2880
GROUP = QUERY_HEADS // KEY_VALUE_HEADS


def dot(a, b):
    return jnp.dot(a, b, preferred_element_type=jnp.float32)


def dot_tn(a, b):
    return lax.dot_general(a, b, (((0,), (0,)), ((), ())), preferred_element_type=jnp.float32)


def dot_nt(a, b):
    return lax.dot_general(a, b, (((1,), (1,)), ((), ())), preferred_element_type=jnp.float32)


def inverse_rms(values):
    return lax.rsqrt(jnp.mean(values * values, axis=-1, keepdims=True) + EPSILON)


def rms_back(values, inv_rms, grad_in):
    inner_mean = jnp.mean(grad_in * values, axis=-1, keepdims=True)
    return inv_rms * grad_in - values * (inv_rms * inv_rms * inv_rms) * inner_mean


def shifted(shard, by):
    size = lax.axis_size(CTX)
    pairs = [(i, i + by) for i in range(size) if 0 <= i + by < size]
    return lax.ppermute(shard, CTX, pairs)


def pad_features(v):
    return jnp.pad(v.reshape(-1, 32, SHARD), ((0, 0), (0, 0), (0, PADDED - SHARD))).reshape(-1, 32 * PADDED)


def drop_padding(v):
    return v.reshape(-1, 32, PADDED)[:, :, :SHARD].reshape(-1, MODEL)


def band_valid(block_idx):
    query_pos = block_idx * 128 + jnp.arange(128)[:, None]
    key_pos = block_idx * 128 - WINDOW + jnp.arange(WINDOW + 128)[None, :]
    return (key_pos <= query_pos) & (key_pos > query_pos - WINDOW) & (key_pos >= 0)


def attend(query, keys, values, valid):
    scores = dot_nt(query, keys) * 0.125
    weights = jnp.where(valid, jnp.exp(scores), 0.0)
    prob = weights / jnp.sum(weights, axis=-1, keepdims=True)
    prob_bf = bf(prob)
    return bf(dot(prob_bf, values)), prob, prob_bf


def attend_back(query, keys, values, prob, prob_bf, grad_out):
    grad_prob = dot_nt(grad_out, values)
    grad_value = dot_tn(prob_bf, grad_out)
    grad_score = bf(
        prob * (grad_prob - jnp.sum(grad_prob * prob, axis=-1, keepdims=True)) * 0.125
    )
    return dot(grad_score, keys), dot_tn(grad_score, query), grad_value


def heads_first(v):
    return v.reshape(128, GROUP, HEAD_SIZE).transpose(1, 0, 2).reshape(GROUP * 128, HEAD_SIZE)


def heads_last(v):
    return v.reshape(GROUP, 128, HEAD_SIZE).transpose(1, 0, 2).reshape(128, GROUP * HEAD_SIZE)


def pack_rows(main_t, extra_t, rows):
    low = dot(main_t, rows[:, :HALF_LANES])
    high = dot(main_t, rows[:, HALF_LANES:])
    padded = jnp.pad(rows, ((0, 0), (0, 192)))
    quarters = jnp.concatenate([padded[:, 768 * q : 768 * q + 768] for q in range(4)], axis=0)
    extra = dot(extra_t, quarters)
    return low, high, extra


def join(low, high, extra):
    second = jnp.concatenate(
        [bf(high), jnp.zeros((512, 64), jnp.bfloat16), bf(extra), jnp.zeros((512, 128), jnp.bfloat16)],
        axis=1,
    )
    return jnp.stack([bf(low), second]).reshape(2, 32, 16, HALF_LANES)


def unpack_rows(packed):
    packed = packed.reshape(2, 512, HALF_LANES)
    main = jnp.concatenate([packed[0], packed[1, :, :960]], axis=1)
    extra = packed[1, :, 1024:1792].reshape(32, 4, 4, 768).transpose(0, 2, 1, 3).reshape(128, 3072)
    return jnp.concatenate([main, extra[:, :MODEL]], axis=0)


def repack_rows(rows):
    main, extra = rows[:512], jnp.pad(rows[512:], ((0, 0), (0, 192)))
    extra = extra.reshape(32, 4, 4, 768).transpose(0, 2, 1, 3).reshape(512, 768)
    zeros = lambda n: jnp.zeros((512, n), jnp.bfloat16)
    second = jnp.concatenate([main[:, HALF_LANES:], zeros(64), extra, zeros(128)], axis=1)
    return jnp.stack([main[:, :HALF_LANES], second]).reshape(2, 32, 16, HALF_LANES)


def combine(main_w, extra_w, back, core):
    back = back.reshape(512, HALF_LANES)
    main = dot(main_w, back)
    extra = [dot(extra_w[:, 512 * q : 512 * q + 512], back[:, 1024:1792]) for q in range(4)]
    extra = jnp.concatenate(extra, axis=1)[:, :MODEL]
    first = jnp.pad(main, ((0, 0), (0, MODEL - HALF_LANES)))
    second = jnp.pad(main[:, :960], ((0, 0), (HALF_LANES, 0))) + extra
    return jnp.where(core == 0, first, second)


def add_base(total, mine, base):
    return bf(f32(base[mine, :]) + total)


def finish_resid(total, mine, cot, resid, grad_resid):
    values = f32(resid[mine, :])
    out = f32(cot[mine, :]) + rms_back(values, inverse_rms(values), total)
    grad_resid[...] = out
    return bf(out)


def finish_tokens(total, mine, tokens, grad_resid):
    values = f32(tokens[mine, :])
    return bf(grad_resid[...] + rms_back(values, inverse_rms(values), total))


def body(
    tokens, cotangent, expert_ids, combine_weights,
    w_query, key_value_weight, w_output, w_gate, w_up, w_down,
):
    ctx_block = lax.axis_index(CTX)
    core = lax.axis_index(EXP) % 2
    tokens_f32 = f32(tokens)
    normed = bf(tokens_f32 * inverse_rms(tokens_f32))
    normed_pad = pad_features(normed)
    shard = jnp.concatenate([w_query, key_value_weight, w_output.T], axis=1)
    full = gather_weights(jnp.pad(shard, ((0, PADDED - SHARD), (0, 0))))

    named = expert_ids[:, :, None] == jnp.arange(32)[None, None, :]
    hot = jnp.any(named, axis=1)
    weight = jnp.sum(jnp.where(named, combine_weights[:, :, None], 0.0), axis=1)
    order = jnp.arange(128)
    earlier = dot(bf(order[:, None] > order[None, :]), bf(hot))
    slots = jnp.arange(512)
    widen = bf(jnp.arange(32)[:, None] == slots[None, :] // 16)
    slot_of = dot(bf(jnp.where(hot, earlier, 64.0)), widen)
    weight_of = jnp.repeat(weight, 16, axis=1)
    is_main = slot_of == f32(slots % 16)[None, :]
    is_extra = slot_of == f32(16 + slots % 4)[None, :]
    quarter = [is_extra & (slots % 16 // 4 == q)[None, :] for q in range(4)]
    main_t = bf(is_main).T
    extra_t = jnp.concatenate([bf(q) for q in quarter], axis=0).T
    main_scale = jnp.sum(jnp.where(is_main, weight_of, 0.0), axis=0)[:, None]
    extra_scale = jnp.sum(jnp.where(is_extra, weight_of, 0.0), axis=0)[:, None]

    low, high, extra = pack_rows(main_t, extra_t, cotangent)
    grad_packed = join(low * main_scale, high * main_scale, extra * extra_scale)

    projected = bf(dot(normed_pad, full[:, :384]))
    query_matrix, key_value = projected[:, :256], projected[:, 256:]
    prev_rim = shifted(key_value, 1)
    span = jnp.concatenate([prev_rim, key_value], axis=0)
    keys, values = span[:, :HEAD_SIZE], span[:, HEAD_SIZE:]
    valid = jnp.tile(band_valid(ctx_block), (GROUP, 1))
    query = heads_first(query_matrix)
    attended, prob, prob_bf = attend(query, keys, values, valid)
    attended = heads_last(attended)
    head_part = bf(drop_padding(dot_nt(attended, full[:, 384:])))
    (residual,) = sum_heads(head_part, add_base, [tokens], 4, name="residual")
    residual_f32 = f32(residual)
    moe_input = bf(residual_f32 * inverse_rms(residual_f32))
    row_packed = join(*pack_rows(main_t, extra_t, moe_input))
    rows, grads = dispatch(row_packed, grad_packed)
    expert_rows, grad_expert = unpack_rows(rows), unpack_rows(grads)

    gate_pre = dot(expert_rows, w_gate[0])
    up_pre = dot(expert_rows, w_up[0])
    gate_sig = jax.nn.sigmoid(GLU_ALPHA * gate_pre)
    gate_glu = gate_pre * gate_sig
    activated = bf(gate_glu * (up_pre + 1.0))
    down_part = bf(dot(activated, w_down[0]))
    grad_act = dot_nt(grad_expert, w_down[0])
    grad_gate_pre = bf(
        grad_act * (up_pre + 1.0) * (gate_sig + GLU_ALPHA * gate_glu * (1.0 - gate_sig))
    )
    grad_up_pre = bf(grad_act * gate_glu)
    grad_down = bf(dot_tn(activated, grad_expert))[None]
    grad_gate = bf(dot_tn(expert_rows, grad_gate_pre))[None]
    grad_up = bf(dot_tn(expert_rows, grad_up_pre))[None]
    input_part = bf(dot_nt(grad_gate_pre, w_gate[0]) + dot_nt(grad_up_pre, w_up[0]))
    input_back, down_back = giveback(repack_rows(input_part), repack_rows(down_part))

    extra_w = extra_t.T
    extra_one = jnp.concatenate([bf(q) for q in quarter], axis=1)
    grad_normed = combine(bf(is_main), extra_one, input_back, core)
    weighted = lambda m: jnp.where(m, weight_of, 0.0)
    whole_w = jnp.concatenate([weighted(is_main)] + [weighted(q) for q in quarter], axis=1)
    high_w = bf(whole_w)
    low_w = bf(whole_w - f32(high_w))
    moe_part = combine(high_w[:, :512], high_w[:, 512:], down_back, core) + combine(
        low_w[:, :512], low_w[:, 512:], down_back, core
    )
    own = jax.ShapeDtypeStruct((16, MODEL), jnp.float32)
    grad_resid_bf, grad_resid = sum_heads(
        bf(grad_normed), finish_resid, [cotangent, residual], 5, (own,), name="grad_residual"
    )
    (block_out,) = sum_heads(bf(moe_part), add_base, [residual], 4, name="block_out")
    resid_pad = pad_features(grad_resid_bf)
    attended_grad = bf(dot(resid_pad, full[:, 384:]))
    query_grads, key_grads, value_grads = attend_back(
        query, keys, values, prob, prob_bf, heads_first(attended_grad)
    )
    span_grads = jnp.concatenate([key_grads, value_grads], axis=1)
    rim_grad = f32(shifted(bf(span_grads[:WINDOW]), -1))
    key_value_grad = bf(span_grads[WINDOW:] + rim_grad)
    query_grad = heads_last(bf(query_grads))
    qkv_grad = jnp.concatenate([query_grad, key_value_grad], axis=1)
    grad_part = bf(drop_padding(dot_nt(qkv_grad, full[:, :384])))
    (grad_tokens,) = sum_heads(grad_part, finish_tokens, [tokens, grad_resid], 6, name="grad_tokens")
    terms = bf(jnp.concatenate([dot_tn(normed_pad, qkv_grad), dot_tn(resid_pad, attended)], axis=1))
    sums = scatter_sums(terms)[:SHARD]
    return (
        block_out, grad_tokens, sums[:, :256], sums[:, 256:384], sums[:, 384:].T,
        grad_gate, grad_up, grad_down,
    )


def solution(mesh):
    in_specs = (
        P("ctx", None), P("ctx", None), P("ctx", None), P("ctx", None),
        P("ctx", "exp"), P("ctx", "exp"), P("exp", "ctx"),
        P("ctx", None, "exp"), P("ctx", None, "exp"), P("ctx", "exp", None),
    )
    out_specs = (
        P("ctx", None), P("ctx", None), P("ctx", "exp"), P("ctx", "exp"), P("exp", "ctx"),
        P("ctx", None, "exp"), P("ctx", None, "exp"), P("ctx", "exp", None),
    )
    return jax.shard_map(body, mesh=mesh, in_specs=in_specs, out_specs=out_specs, check_vma=False)
```

```python
import functools

import jax
import jax.numpy as jnp
from jax import lax
from jax.experimental import pallas as pl
from jax.experimental.pallas import tpu as pltpu
from jax.sharding import PartitionSpec as P

CTX, EXP = "ctx", "exp"
SHARD = 90
PADDED = 96
HALF_LANES = 1920
MESH = pl.DeviceIdType.MESH
VMEM_BYTES = 60 * 2**20


def params(collective_id):
    return pltpu.CompilerParams(
        collective_id=collective_id, has_side_effects=True, vmem_limit_bytes=VMEM_BYTES
    )


def vmem_specs(count):
    return [pl.BlockSpec(memory_space=pltpu.VMEM)] * count


def place():
    c = lax.axis_index(CTX)
    return c, c // 16, (c // 4) % 4, c % 4


def greet(peers):
    barrier = pltpu.get_barrier_semaphore()
    for peer in peers:
        pl.semaphore_signal(barrier, inc=1, device_id=peer, device_id_type=MESH)
    pl.semaphore_wait(barrier, len(peers))


def gather_kernel(w_ref, out_ref, send, recv):
    c, z, y, x = place()
    e = lax.axis_index(EXP)

    def dev(zz, yy, xx):
        return (zz * 16 + ((yy + 4) % 4) * 4 + (xx + 4) % 4, e)

    def copy(n, src, dst, to):
        cp = pltpu.make_async_remote_copy(
            src_ref=src, dst_ref=dst, send_sem=send.at[n], recv_sem=recv.at[n],
            device_id=to, device_id_type=MESH,
        )
        cp.start()
        return cp

    greet([dev(1 - z, y, x), dev(z, y + 1, x), dev(z, y - 1, x), dev(z, y, x + 1), dev(z, y, x - 1)])
    rows = (pl.ds(0, 48), pl.ds(48, 48))
    copies = []
    first = []
    for h in range(2):
        first.append(copy(h, w_ref.at[rows[h]], out_ref.at[z, y, x, rows[h]], dev(1 - z, y, x)))
    out_ref[z, y, x] = w_ref[...]
    copies += first

    def view(h, phase, zsel, pos):
        along_x = (h == 0) == (phase == 1)
        if phase == 1:
            return out_ref.at[zsel, y, pos, rows[h]] if along_x else out_ref.at[zsel, pos, x, rows[h]]
        return out_ref.at[zsel, :, pos, rows[h]] if along_x else out_ref.at[zsel, pos, :, rows[h]]

    def ring(h, phase):
        along_x = (h == 0) == (phase == 1)
        me = x if along_x else y
        up = dev(z, y, x + 1) if along_x else dev(z, y + 1, x)
        down = dev(z, y, x - 1) if along_x else dev(z, y - 1, x)
        return me, (me + 3) % 4, (me + 1) % 4, up, down

    for phase in (1, 2):
        direct = []
        for h in range(2):
            for cp in first[h] if phase == 2 else (first[h],):
                cp.wait_recv()
            me, low, high, up, down = ring(h, phase)
            n = 2 + (phase - 1) * 8 + h * 4
            both = pl.ds(0, 2)
            direct.append((
                copy(n, view(h, phase, both, me), view(h, phase, both, me), up),
                copy(n + 1, view(h, phase, both, me), view(h, phase, both, me), down),
            ))
        later = []
        for h in range(2):
            me, low, high, up, down = ring(h, phase)
            n = 2 + (phase - 1) * 8 + h * 4
            direct[h][0].wait_recv()
            a = copy(n + 2, view(h, phase, 0, low), view(h, phase, 0, low), up)
            direct[h][1].wait_recv()
            b = copy(n + 3, view(h, phase, 1, high), view(h, phase, 1, high), down)
            later.append((a, b))
        for h in range(2):
            copies += [*direct[h], *later[h]]
        first = later
    for h in range(2):
        for cp in first[h]:
            cp.wait_recv()
    for cp in copies:
        cp.wait_send()


def gather_weights(shard):
    out = pl.pallas_call(
        gather_kernel,
        out_shape=jax.ShapeDtypeStruct((2, 4, 4, PADDED, 640), jnp.bfloat16),
        in_specs=vmem_specs(1),
        out_specs=vmem_specs(1)[0],
        scratch_shapes=[pltpu.SemaphoreType.DMA((18,)), pltpu.SemaphoreType.DMA((18,))],
        compiler_params=params(0),
        name="gather_weights",
    )(shard)
    return out.reshape(32 * PADDED, 640)


def f32(v):
    return v.astype(jnp.float32)


def bf(v):
    return v.astype(jnp.bfloat16)


def scatter_kernel(t_ref, out_ref, far, near, stage, acc1, far2, near2, stage2, acc2, last, send, recv):
    c, z, y, x = place()
    e = lax.axis_index(EXP)

    def dev(zz, yy, xx):
        return (zz * 16 + ((yy + 4) % 4) * 4 + (xx + 4) % 4, e)

    def copy(n, src, dst, to):
        cp = pltpu.make_async_remote_copy(
            src_ref=src, dst_ref=dst, send_sem=send.at[n], recv_sem=recv.at[n],
            device_id=to, device_id_type=MESH,
        )
        cp.start()
        return cp

    greet([dev(1 - z, y, x), dev(z, y + 1, x), dev(z, y - 1, x), dev(z, y, x + 1), dev(z, y, x - 1)])
    rows = (pl.ds(0, 48), pl.ds(48, 48))
    copies = []

    def ring(along_x):
        me = x if along_x else y
        up = dev(z, y, x + 1) if along_x else dev(z, y + 1, x)
        down = dev(z, y, x - 1) if along_x else dev(z, y - 1, x)
        return me, (me + 3) % 4, (me + 1) % 4, (me + 2) % 4, up, down

    def step(phase, source, far_ref, near_ref, stage_ref):
        started = []
        for h in range(2):
            me, low, high, across, up, down = ring((h == 1) == (phase == 1))
            n = (phase - 1) * 12 + h * 6
            started.append([
                copy(n, source(h, 0, across), far_ref.at[h, 0], up),
                copy(n + 1, source(h, 1, across), far_ref.at[h, 1], down),
                copy(n + 2, source(h, 1, high), near_ref.at[h, 0, 1], up),
                copy(n + 3, source(h, 0, low), near_ref.at[h, 1, 0], down),
            ])
        for h in range(2):
            me, low, high, across, up, down = ring((h == 1) == (phase == 1))
            n = (phase - 1) * 12 + h * 6
            started[h][0].wait_recv()
            stage_ref[h, 0] = bf(f32(source(h, 0, high)[...]) + f32(far_ref[h, 0]))
            started[h].append(copy(n + 4, stage_ref.at[h, 0], near_ref.at[h, 0, 0], up))
            started[h][1].wait_recv()
            stage_ref[h, 1] = bf(f32(source(h, 1, low)[...]) + f32(far_ref[h, 1]))
            started[h].append(copy(n + 5, stage_ref.at[h, 1], near_ref.at[h, 1, 1], down))
        return started

    def first_source(h, zsel, pos):
        return t_ref.at[zsel, pos, :, rows[h]] if h == 0 else t_ref.at[zsel, :, pos, rows[h]]

    started = step(1, first_source, far, near, stage)
    for h in range(2):
        me = ring(h == 1)[0]
        for i in (2, 3, 4, 5):
            started[h][i].wait_recv()
        for zz in range(2):
            acc1[h, zz] = bf(f32(first_source(h, zz, me)[...]) + f32(near[h, 0, zz]) + f32(near[h, 1, zz]))
        copies += started[h]

    def second_source(h, zsel, pos):
        return acc1.at[h, zsel, pos]

    started = step(2, second_source, far2, near2, stage2)
    final = []
    for h in range(2):
        me = ring(h == 0)[0]
        for i in (2, 3, 4, 5):
            started[h][i].wait_recv()
        for zz in range(2):
            acc2[h, zz] = bf(f32(second_source(h, zz, me)[...]) + f32(near2[h, 0, zz]) + f32(near2[h, 1, zz]))
        copies += started[h]
        final.append(copy(24 + h, acc2.at[h, 1 - z], last.at[h], dev(1 - z, y, x)))
    for h in range(2):
        final[h].wait_recv()
        out_ref[rows[h], :] = bf(f32(acc2[h, z]) + f32(last[h]))
    for cp in copies + final:
        cp.wait_send()


def scatter_sums(terms):
    b = jnp.bfloat16
    return pl.pallas_call(
        scatter_kernel,
        out_shape=jax.ShapeDtypeStruct((PADDED, 640), b),
        in_specs=vmem_specs(1),
        out_specs=vmem_specs(1)[0],
        scratch_shapes=[
            pltpu.VMEM((2, 2, 4, 48, 640), b),
            pltpu.VMEM((2, 2, 2, 4, 48, 640), b),
            pltpu.VMEM((2, 2, 4, 48, 640), b),
            pltpu.VMEM((2, 2, 4, 48, 640), b),
            pltpu.VMEM((2, 2, 48, 640), b),
            pltpu.VMEM((2, 2, 2, 48, 640), b),
            pltpu.VMEM((2, 2, 48, 640), b),
            pltpu.VMEM((2, 2, 48, 640), b),
            pltpu.VMEM((2, 48, 640), b),
            pltpu.SemaphoreType.DMA((26,)),
            pltpu.SemaphoreType.DMA((26,)),
        ],
        compiler_params=params(1),
        name="scatter_sums",
    )(terms.reshape(2, 4, 4, PADDED, 640))


def sum_kernel(post, extra_in, extra_out, *refs):
    part = refs[0]
    ins = refs[1 : 1 + extra_in]
    out = refs[1 + extra_in]
    outs = refs[2 + extra_in : 2 + extra_in + extra_out]
    mate, stage, got, send, recv = refs[2 + extra_in + extra_out :]
    c = lax.axis_index(CTX)
    e = lax.axis_index(EXP)
    h, k = e // 2, e % 2
    partner = (c, e + 1 - 2 * k)

    def peer(d):
        return (c, ((h + d) % 4) * 2 + k)

    greet([partner, peer(1), peer(2), peer(3)])

    def rows(core, block):
        return pl.ds(pl.multiple_of(core * 64 + block * 16, 16), 16)

    def copy(n, src, dst, to):
        cp = pltpu.make_async_remote_copy(
            src_ref=src, dst_ref=dst, send_sem=send.at[n], recv_sem=recv.at[n],
            device_id=to, device_id_type=MESH,
        )
        cp.start()
        return cp

    order = (2, 1, 3, 0)
    copies, pair, far = [], {}, {}
    for d in order:
        b = (h + d) % 4
        pair[d] = copy(d, part.at[rows(1 - k, b)], mate.at[b], partner)
    for d in order:
        b = (h + d) % 4
        pair[d].wait_recv()
        both = f32(part[rows(k, b), :]) + f32(mate[b])
        if d:
            stage[d - 1] = bf(both)
            far[d] = copy(4 + d, stage.at[d - 1], got.at[d - 1], peer(d))
    total = both
    for d in (1, 3, 2):
        far[d].wait_recv()
        total = total + f32(got[d - 1])
    mine = rows(k, h)
    out[mine, :] = post(total, mine, *ins, *outs)
    spread = {d: copy(8 + d, out.at[mine], out.at[mine], peer(d)) for d in (2, 1, 3)}
    passed = [copy(12, out.at[mine], out.at[mine], partner)]
    for d in (1, 3, 2):
        spread[d].wait_recv()
        theirs = rows(k, (h - d + 4) % 4)
        passed.append(copy(12 + d, out.at[theirs], out.at[theirs], partner))
    for cp in passed:
        cp.wait_recv()
    for cp in [*pair.values(), *far.values(), *spread.values(), *passed]:
        cp.wait_send()


def sum_heads(part, post, ins, collective_id, extra_outs=(), name="sum_heads"):
    b = jnp.bfloat16
    width = part.shape[1]
    res = pl.pallas_call(
        functools.partial(sum_kernel, post, len(ins), len(extra_outs)),
        out_shape=[jax.ShapeDtypeStruct((128, width), b), *extra_outs],
        in_specs=vmem_specs(1 + len(ins)),
        out_specs=vmem_specs(1 + len(extra_outs)),
        scratch_shapes=[
            pltpu.VMEM((4, 16, width), b),
            pltpu.VMEM((3, 16, width), b),
            pltpu.VMEM((3, 16, width), b),
            pltpu.SemaphoreType.DMA((16,)),
            pltpu.SemaphoreType.DMA((16,)),
        ],
        compiler_params=params(collective_id),
        name=name,
    )(part, *ins)
    return res


EPSILON = 1e-05
GLU_ALPHA = 1.702
QUERY_HEADS = 32
KEY_VALUE_HEADS = 8
HEAD_SIZE = 64
WINDOW = 128
MODEL = 2880
GROUP = QUERY_HEADS // KEY_VALUE_HEADS


def dot(a, b):
    return jnp.dot(a, b, preferred_element_type=jnp.float32)


def dot_tn(a, b):
    return lax.dot_general(a, b, (((0,), (0,)), ((), ())), preferred_element_type=jnp.float32)


def dot_nt(a, b):
    return lax.dot_general(a, b, (((1,), (1,)), ((), ())), preferred_element_type=jnp.float32)


def inverse_rms(values):
    return lax.rsqrt(jnp.mean(values * values, axis=-1, keepdims=True) + EPSILON)


def rms_back(values, inv_rms, grad_in):
    inner_mean = jnp.mean(grad_in * values, axis=-1, keepdims=True)
    return inv_rms * grad_in - values * (inv_rms * inv_rms * inv_rms) * inner_mean


def shifted(shard, by):
    size = lax.axis_size(CTX)
    pairs = [(i, i + by) for i in range(size) if 0 <= i + by < size]
    return lax.ppermute(shard, CTX, pairs)


def pad_features(v):
    return jnp.pad(v.reshape(-1, 32, SHARD), ((0, 0), (0, 0), (0, PADDED - SHARD))).reshape(-1, 32 * PADDED)


def drop_padding(v):
    return v.reshape(-1, 32, PADDED)[:, :, :SHARD].reshape(-1, MODEL)


def band_valid(block_idx):
    query_pos = block_idx * 128 + jnp.arange(128)[:, None]
    key_pos = block_idx * 128 - WINDOW + jnp.arange(WINDOW + 128)[None, :]
    return (key_pos <= query_pos) & (key_pos > query_pos - WINDOW) & (key_pos >= 0)


def attend(query, keys, values, valid):
    scores = dot_nt(query, keys) * 0.125
    weights = jnp.where(valid, jnp.exp(scores), 0.0)
    prob = weights / jnp.sum(weights, axis=-1, keepdims=True)
    prob_bf = bf(prob)
    return bf(dot(prob_bf, values)), prob, prob_bf


def attend_back(query, keys, values, prob, prob_bf, grad_out):
    grad_prob = dot_nt(grad_out, values)
    grad_value = dot_tn(prob_bf, grad_out)
    grad_score = bf(
        prob * (grad_prob - jnp.sum(grad_prob * prob, axis=-1, keepdims=True)) * 0.125
    )
    return dot(grad_score, keys), dot_tn(grad_score, query), grad_value


def heads_first(v):
    return v.reshape(128, GROUP, HEAD_SIZE).transpose(1, 0, 2).reshape(GROUP * 128, HEAD_SIZE)


def heads_last(v):
    return v.reshape(GROUP, 128, HEAD_SIZE).transpose(1, 0, 2).reshape(128, GROUP * HEAD_SIZE)


def iota(shape, axis):
    return lax.broadcasted_iota(jnp.int32, shape, axis)


def spread_extra(q):
    r, j = iota((128, 512), 0), iota((128, 512), 1)
    return bf((j == (r // 4) * 16 + q * 4 + r % 4).astype(jnp.float32))


def expert_kernel(
    x_ref, cot_ref, ids_ref, combine_ref, wg, wu, wd,
    grad_in_part, moe_part, grad_gate, grad_up, grad_down,
    xp, one_hot, extra_hot, weight_ref, scale, send_buf, got, ext, gate_pre, up_pre, act, gg, gu, parts, other, back,
    send, recv, send2, recv2, send3, recv3, send4, recv4,
):
    c = lax.axis_index(CTX)
    e = lax.axis_index(EXP)
    k = e % 2
    partner = (c, e + 1 - 2 * k)
    group, inner = c // 8, c % 8
    barrier = pltpu.get_barrier_semaphore()

    def moved(n, sign):
        return ((group + sign * (n // 8) + 4) % 4) * 8 + (inner + sign * (n % 8) + 8) % 8

    def hello(n, t):
        pl.semaphore_signal(barrier, inc=1, device_id=(moved(n, 1), e), device_id_type=MESH)
        return t

    lax.fori_loop(1, 32, hello, 0)
    pl.semaphore_signal(barrier, inc=1, device_id=partner, device_id_type=MESH)

    lane = iota((128, 512), 1)
    hot = jnp.zeros((128, 512), jnp.float32)
    weight = jnp.zeros((128, 512), jnp.float32)
    for route in range(4):
        match = ids_ref[:, route : route + 1] == lane // 16
        hot = jnp.where(match, 1.0, hot)
        weight = jnp.where(match, combine_ref[:, route : route + 1], weight)
    weight_ref[...] = weight
    below = bf(jnp.where(iota((128, 128), 0) > iota((128, 128), 1), 1.0, 0.0))
    slot = jnp.where(hot > 0, dot(below, bf(hot)), 64.0)
    main = slot == f32(lane % 16)
    extra = slot == f32(16 + lane % 4)
    one_hot[...] = bf(jnp.where(main, 1.0, 0.0))
    for q in range(4):
        extra_hot[q] = bf(jnp.where(extra & (lane % 16 // 4 == q), 1.0, 0.0))
    scale[0] = jnp.sum(jnp.where(main, weight, 0.0).T, axis=1, keepdims=True)
    scale[1] = jnp.sum(jnp.where(extra, weight, 0.0).T, axis=1, keepdims=True)
    for a, ref in enumerate((x_ref, cot_ref)):
        xp[a, :, :MODEL] = ref[...]
        xp[a, :, MODEL:] = jnp.zeros((128, 192), jnp.bfloat16)

    def out_copy(a, n):
        to = moved(n, 1)
        return pltpu.make_async_remote_copy(
            src_ref=send_buf.at[a, to], dst_ref=got.at[a, k, c],
            send_sem=send.at[a, n], recv_sem=recv.at[a, n],
            device_id=(to, e), device_id_type=MESH,
        )

    def over(a, n):
        source = moved(n, -1)
        return pltpu.make_async_remote_copy(
            src_ref=got.at[a, k, source], dst_ref=got.at[a, k, source],
            send_sem=send2.at[a, n], recv_sem=recv2.at[a, n],
            device_id=partner, device_id_type=MESH,
        )

    def pack(a, j, t):
        g = (group + j) % 4
        at = pl.ds(pl.multiple_of(g * 128, 128), 128)
        dest = pl.ds(g * 8, 8)
        m = one_hot[:, at]
        s0 = scale[0, at, :] if a else 1.0
        s1 = scale[1, at, :] if a else 1.0

        @pl.when(k == 0)
        def _():
            low = dot_tn(m, xp[a, :, :HALF_LANES])
            send_buf[a, dest] = bf(low * s0 if a else low).reshape(8, 16, HALF_LANES)

        @pl.when(k == 1)
        def _():
            high = dot_tn(m, xp[a, :, HALF_LANES:2944])
            send_buf[a, dest, :, 0:1024] = bf(high * s0 if a else high).reshape(8, 16, 1024)
            quarters = dot_tn(extra_hot[0, :, at], xp[a, :, 0:768])
            for q in range(1, 4):
                quarters = quarters + dot_tn(extra_hot[q, :, at], xp[a, :, 768 * q : 768 * q + 768])
            send_buf[a, dest, :, 1024:1792] = bf(quarters * s1 if a else quarters).reshape(8, 16, 768)
            send_buf[a, dest, :, 1792:] = jnp.zeros((8, 16, 128), jnp.bfloat16)

        return t

    def start_group(a, j):
        first = 1 if j == 0 else 0
        lax.fori_loop(first, 8, lambda i, t: (out_copy(a, j * 8 + i).start(), t)[1], 0)

    for a in range(2):
        for j in range(4):
            pack(a, j, 0)
            if a == 0 and j == 0:
                pl.semaphore_wait(barrier, 32)
            start_group(a, j)
        got[a, k, c] = send_buf[a, c]
        over(a, 0).start()

    def arrived(a, n, t):
        out_copy(a, n).wait_recv()
        over(a, n).start()
        return t

    def take(a):
        lax.fori_loop(1, 32, lambda n, t: arrived(a, n, t), 0)
        lax.fori_loop(0, 32, lambda n, t: (over(a, n).wait(), t)[1], 0)
        packed = got[a, 1, :, :, 1024:1792].reshape(512, 768)
        for q in range(4):
            ext[a, :, 768 * q : 768 * q + 768] = bf(dot(spread_extra(q), packed))

    def rows_of(a, t):
        first = got[a, 0, pl.ds(t * 16, 16)].reshape(256, HALF_LANES)
        second = got[a, 1, pl.ds(t * 16, 16), :, 0:960].reshape(256, 960)
        return first, second

    def at_rows(t):
        return pl.ds(pl.multiple_of(t * 256, 256), 256)

    take(0)

    def forward(t, carry):
        first, second = rows_of(0, t)
        for w, into in ((wg, gate_pre), (wu, up_pre)):
            into[at_rows(t), :] = dot(first, w[:HALF_LANES]) + dot(second, w[HALF_LANES:])
        return carry

    lax.fori_loop(0, 2, forward, 0)
    for w, into in ((wg, gate_pre), (wu, up_pre)):
        into[512:, :] = dot(ext[0, :, :MODEL], w[...])

    take(1)

    def pointwise(rows, grad_act):
        gate, up = gate_pre[rows, :], up_pre[rows, :] + 1.0
        sig = jax.nn.sigmoid(GLU_ALPHA * gate)
        glu = gate * sig
        act[rows, :] = bf(glu * up)
        gg[rows, :] = bf(grad_act * up * (sig + GLU_ALPHA * glu * (1.0 - sig)))
        gu[rows, :] = bf(grad_act * glu)

    def backward(t, carry):
        first, second = rows_of(1, t)
        pointwise(at_rows(t), dot_nt(first, wd[:, :HALF_LANES]) + dot_nt(second, wd[:, HALF_LANES:]))
        return carry

    lax.fori_loop(0, 2, backward, 0)
    pointwise(pl.ds(512, 128), dot_nt(ext[1, :, :MODEL], wd[...]))

    for a in range(2):
        lax.fori_loop(1, 32, lambda n, t, a=a: (out_copy(a, n).wait_send(), t)[1], 0)

    def across(a, j):
        block = pl.ds(((group + j) % 4) * 8, 8)
        return pltpu.make_async_remote_copy(
            src_ref=parts.at[a, 1 - k, block], dst_ref=other.at[a, block],
            send_sem=send3.at[a, j], recv_sem=recv3.at[a, j],
            device_id=partner, device_id_type=MESH,
        )

    def home(a, n):
        to = moved(n, 1)
        return pltpu.make_async_remote_copy(
            src_ref=send_buf.at[a, to], dst_ref=back.at[a, c],
            send_sem=send4.at[a, n], recv_sem=recv4.at[a, n],
            device_id=(to, e), device_id_type=MESH,
        )

    def result(a, rows):
        if a == 0:
            return bf(dot_nt(gg[rows, :], wg[...]) + dot_nt(gu[rows, :], wu[...]))
        return bf(dot(act[rows, :], wd[...]))

    def add_pair(a, j):
        across(a, j).wait_recv()

        def one(i, t):
            n = j * 8 + i
            to = moved(n, 1)
            send_buf[a, to] = bf(f32(parts[a, k, to]) + f32(other[a, to]))

            @pl.when(n > 0)
            def _():
                home(a, n).start()

            return t

        lax.fori_loop(0, 8, one, 0)
        if j == 0:
            back[a, c] = send_buf[a, c]

    steps = [(a, j) for a in range(2) for j in range(4)]
    for index, (a, j) in enumerate(steps):
        if j == 0:
            last = result(a, pl.ds(512, 128))
            folded = jnp.zeros((512, 768), jnp.float32)
            for q in range(4):
                width = 768 if q < 3 else 576
                piece = dot_tn(spread_extra(q), last[:, 768 * q : 768 * q + width])
                if q == 3:
                    piece = jnp.concatenate([piece, jnp.zeros((512, 192), jnp.float32)], axis=1)
                folded = folded + piece
            parts[a, 1, :, :, 1024:1792] = bf(folded).reshape(32, 16, 768)
            parts[a, 1, :, :, 960:1024] = jnp.zeros((32, 16, 64), jnp.bfloat16)
            parts[a, 1, :, :, 1792:] = jnp.zeros((32, 16, 128), jnp.bfloat16)
        g = (group + j) % 4
        rows = result(a, pl.ds(pl.multiple_of(g * 128, 128), 128))
        parts[a, 0, pl.ds(g * 8, 8)] = rows[:, :HALF_LANES].reshape(8, 16, HALF_LANES)
        parts[a, 1, pl.ds(g * 8, 8), :, 0:960] = rows[:, HALF_LANES:].reshape(8, 16, 960)
        across(a, j).start()
        if index:
            add_pair(*steps[index - 1])
    add_pair(*steps[-1])

    def grads_at(columns, lanes, half):
        x_main = got[0, half, :, :, lanes].reshape(512, lanes.size)
        g_main = got[1, half, :, :, lanes].reshape(512, lanes.size)
        x_ext, g_ext = ext[0, :, columns], ext[1, :, columns]
        grad_gate[columns, :] = bf(dot_tn(x_main, gg[:512, :]) + dot_tn(x_ext, gg[512:, :]))
        grad_up[columns, :] = bf(dot_tn(x_main, gu[:512, :]) + dot_tn(x_ext, gu[512:, :]))
        grad_down[:, columns] = bf(dot_tn(act[:512, :], g_main) + dot_tn(act[512:, :], g_ext))

    def lower(i, t):
        lanes = pl.ds(pl.multiple_of(i * 384, 128), 384)
        grads_at(lanes, lanes, 0)
        return t

    lax.fori_loop(0, 5, lower, 0)
    grads_at(pl.ds(1920, 512), pl.ds(0, 512), 1)
    grads_at(pl.ds(2432, 448), pl.ds(512, 448), 1)

    for a, into in enumerate((grad_in_part, moe_part)):
        lax.fori_loop(1, 32, lambda n, t, a=a: (home(a, n).wait_recv(), t)[1], 0)

        def summed(hot, lanes, a=a):
            rows = back[a, :, :, lanes].reshape(512, lanes.size)
            if a == 0:
                return dot(hot, rows)
            spread = jnp.where(hot > 0, weight_ref[...], 0.0)
            high = bf(spread)
            return dot(high, rows) + dot(bf(spread - f32(high)), rows)

        @pl.when(k == 0)
        def _(into=into, summed=summed):
            into[:, :HALF_LANES] = bf(summed(one_hot[...], pl.ds(0, HALF_LANES)))
            into[:, HALF_LANES:] = jnp.zeros((128, 960), jnp.bfloat16)

        @pl.when(k == 1)
        def _(into=into, summed=summed):
            upper = summed(one_hot[...], pl.ds(0, 1024))
            quarters = [summed(extra_hot[q], pl.ds(1024, 768)) for q in range(4)]
            into[:, 0:768] = bf(quarters[0])
            into[:, 768:1536] = bf(quarters[1])
            into[:, 1536:1920] = bf(quarters[2][:, :384])
            into[:, 1920:2304] = bf(quarters[2][:, 384:] + upper[:, :384])
            into[:, 2304:] = bf(quarters[3][:, :576] + upper[:, 384:960])

    for a in range(2):
        lax.fori_loop(1, 32, lambda n, t, a=a: (home(a, n).wait_send(), t)[1], 0)
        lax.fori_loop(0, 4, lambda j, t, a=a: (across(a, j).wait_send(), t)[1], 0)


def experts(moe_input, cotangent, expert_ids, combine_weights, w_gate, w_up, w_down):
    b = jnp.bfloat16
    shape = jax.ShapeDtypeStruct
    return pl.pallas_call(
        expert_kernel,
        out_shape=[
            shape((128, MODEL), b), shape((128, MODEL), b),
            shape((MODEL, 256), b), shape((MODEL, 256), b), shape((256, MODEL), b),
        ],
        in_specs=vmem_specs(7),
        out_specs=vmem_specs(5),
        scratch_shapes=[
            pltpu.VMEM((2, 128, 3072), b),
            pltpu.VMEM((128, 512), b),
            pltpu.VMEM((4, 128, 512), b),
            pltpu.VMEM((128, 512), jnp.float32),
            pltpu.VMEM((2, 512, 1), jnp.float32),
            pltpu.VMEM((2, 32, 16, HALF_LANES), b),
            pltpu.VMEM((2, 2, 32, 16, HALF_LANES), b),
            pltpu.VMEM((2, 128, 3072), b),
            pltpu.VMEM((640, 256), jnp.float32),
            pltpu.VMEM((640, 256), jnp.float32),
            pltpu.VMEM((640, 256), b),
            pltpu.VMEM((640, 256), b),
            pltpu.VMEM((640, 256), b),
            pltpu.VMEM((2, 2, 32, 16, HALF_LANES), b),
            pltpu.VMEM((2, 32, 16, HALF_LANES), b),
            pltpu.VMEM((2, 32, 16, HALF_LANES), b),
        ] + [pltpu.SemaphoreType.DMA((2, 32))] * 4
        + [pltpu.SemaphoreType.DMA((2, 4))] * 2 + [pltpu.SemaphoreType.DMA((2, 32))] * 2,
        compiler_params=params(2),
        name="experts",
    )(moe_input, cotangent, expert_ids, combine_weights, w_gate, w_up, w_down)


def add_base(total, mine, base):
    return bf(f32(base[mine, :]) + total)


def finish_resid(total, mine, cot, resid, grad_resid):
    values = f32(resid[mine, :])
    out = f32(cot[mine, :]) + rms_back(values, inverse_rms(values), total)
    grad_resid[...] = out
    return bf(out)


def finish_tokens(total, mine, tokens, grad_resid):
    values = f32(tokens[mine, :])
    return bf(grad_resid[...] + rms_back(values, inverse_rms(values), total))


def body(
    tokens, cotangent, expert_ids, combine_weights,
    w_query, key_value_weight, w_output, w_gate, w_up, w_down,
):
    ctx_block = lax.axis_index(CTX)
    tokens_f32 = f32(tokens)
    normed = bf(tokens_f32 * inverse_rms(tokens_f32))
    normed_pad = pad_features(normed)
    shard = jnp.concatenate([w_query, key_value_weight, w_output.T], axis=1)
    full = gather_weights(jnp.pad(shard, ((0, PADDED - SHARD), (0, 0))))

    projected = bf(dot(normed_pad, full[:, :384]))
    query_matrix, key_value = projected[:, :256], projected[:, 256:]
    prev_rim = shifted(key_value, 1)
    span = jnp.concatenate([prev_rim, key_value], axis=0)
    keys, values = span[:, :HEAD_SIZE], span[:, HEAD_SIZE:]
    valid = jnp.tile(band_valid(ctx_block), (GROUP, 1))
    query = heads_first(query_matrix)
    attended, prob, prob_bf = attend(query, keys, values, valid)
    attended = heads_last(attended)
    head_part = bf(drop_padding(dot_nt(attended, full[:, 384:])))
    (residual,) = sum_heads(head_part, add_base, [tokens], 4, name="residual")
    residual_f32 = f32(residual)
    moe_input = bf(residual_f32 * inverse_rms(residual_f32))
    grad_normed, moe_part, grad_gate, grad_up, grad_down = experts(
        moe_input, cotangent, expert_ids, combine_weights, w_gate[0], w_up[0], w_down[0]
    )
    own = jax.ShapeDtypeStruct((16, MODEL), jnp.float32)
    grad_resid_bf, grad_resid = sum_heads(
        grad_normed, finish_resid, [cotangent, residual], 5, (own,), name="grad_residual"
    )
    (block_out,) = sum_heads(moe_part, add_base, [residual], 4, name="block_out")
    resid_pad = pad_features(grad_resid_bf)
    attended_grad = bf(dot(resid_pad, full[:, 384:]))
    query_grads, key_grads, value_grads = attend_back(
        query, keys, values, prob, prob_bf, heads_first(attended_grad)
    )
    span_grads = jnp.concatenate([key_grads, value_grads], axis=1)
    rim_grad = f32(shifted(bf(span_grads[:WINDOW]), -1))
    key_value_grad = bf(span_grads[WINDOW:] + rim_grad)
    query_grad = heads_last(bf(query_grads))
    qkv_grad = jnp.concatenate([query_grad, key_value_grad], axis=1)
    grad_part = bf(drop_padding(dot_nt(qkv_grad, full[:, :384])))
    (grad_tokens,) = sum_heads(grad_part, finish_tokens, [tokens, grad_resid], 6, name="grad_tokens")
    terms = bf(jnp.concatenate([dot_tn(normed_pad, qkv_grad), dot_tn(resid_pad, attended)], axis=1))
    sums = scatter_sums(terms)[:SHARD]
    return (
        block_out, grad_tokens, sums[:, :256], sums[:, 256:384], sums[:, 384:].T,
        grad_gate[None], grad_up[None], grad_down[None],
    )


def solution(mesh):
    in_specs = (
        P("ctx", None), P("ctx", None), P("ctx", None), P("ctx", None),
        P("ctx", "exp"), P("ctx", "exp"), P("exp", "ctx"),
        P("ctx", None, "exp"), P("ctx", None, "exp"), P("ctx", "exp", None),
    )
    out_specs = (
        P("ctx", None), P("ctx", None), P("ctx", "exp"), P("ctx", "exp"), P("exp", "ctx"),
        P("ctx", None, "exp"), P("ctx", None, "exp"), P("ctx", "exp", None),
    )
    return jax.shard_map(body, mesh=mesh, in_specs=in_specs, out_specs=out_specs, check_vma=False)
```

```python
import functools

import jax
import jax.numpy as jnp
from jax import lax
from jax.experimental import pallas as pl
from jax.experimental.pallas import tpu as pltpu
from jax.sharding import PartitionSpec as P

CTX, EXP = "ctx", "exp"
SHARD = 90
PADDED = 96
HALF_LANES = 1920
MESH = pl.DeviceIdType.MESH
VMEM_BYTES = 60 * 2**20


def params(collective_id):
    return pltpu.CompilerParams(
        collective_id=collective_id, has_side_effects=True, vmem_limit_bytes=VMEM_BYTES
    )


def vmem_specs(count):
    return [pl.BlockSpec(memory_space=pltpu.VMEM)] * count


def place():
    c = lax.axis_index(CTX)
    return c, c // 16, (c // 4) % 4, c % 4


def greet(peers):
    barrier = pltpu.get_barrier_semaphore()
    for peer in peers:
        pl.semaphore_signal(barrier, inc=1, device_id=peer, device_id_type=MESH)
    pl.semaphore_wait(barrier, len(peers))


def gather_kernel(w_ref, out_ref, send, recv):
    c, z, y, x = place()
    e = lax.axis_index(EXP)

    def dev(zz, yy, xx):
        return (zz * 16 + ((yy + 4) % 4) * 4 + (xx + 4) % 4, e)

    def copy(n, src, dst, to):
        cp = pltpu.make_async_remote_copy(
            src_ref=src, dst_ref=dst, send_sem=send.at[n], recv_sem=recv.at[n],
            device_id=to, device_id_type=MESH,
        )
        cp.start()
        return cp

    greet([dev(1 - z, y, x), dev(z, y + 1, x), dev(z, y - 1, x), dev(z, y, x + 1), dev(z, y, x - 1)])
    rows = (pl.ds(0, 48), pl.ds(48, 48))
    copies = []
    first = []
    for h in range(2):
        first.append(copy(h, w_ref.at[rows[h]], out_ref.at[z, y, x, rows[h]], dev(1 - z, y, x)))
    out_ref[z, y, x] = w_ref[...]
    copies += first

    def view(h, phase, zsel, pos):
        along_x = (h == 0) == (phase == 1)
        if phase == 1:
            return out_ref.at[zsel, y, pos, rows[h]] if along_x else out_ref.at[zsel, pos, x, rows[h]]
        return out_ref.at[zsel, :, pos, rows[h]] if along_x else out_ref.at[zsel, pos, :, rows[h]]

    def ring(h, phase):
        along_x = (h == 0) == (phase == 1)
        me = x if along_x else y
        up = dev(z, y, x + 1) if along_x else dev(z, y + 1, x)
        down = dev(z, y, x - 1) if along_x else dev(z, y - 1, x)
        return me, (me + 3) % 4, (me + 1) % 4, up, down

    for phase in (1, 2):
        direct = []
        for h in range(2):
            for cp in first[h] if phase == 2 else (first[h],):
                cp.wait_recv()
            me, low, high, up, down = ring(h, phase)
            n = 2 + (phase - 1) * 8 + h * 4
            both = pl.ds(0, 2)
            direct.append((
                copy(n, view(h, phase, both, me), view(h, phase, both, me), up),
                copy(n + 1, view(h, phase, both, me), view(h, phase, both, me), down),
            ))
        later = []
        for h in range(2):
            me, low, high, up, down = ring(h, phase)
            n = 2 + (phase - 1) * 8 + h * 4
            direct[h][0].wait_recv()
            a = copy(n + 2, view(h, phase, 0, low), view(h, phase, 0, low), up)
            direct[h][1].wait_recv()
            b = copy(n + 3, view(h, phase, 1, high), view(h, phase, 1, high), down)
            later.append((a, b))
        for h in range(2):
            copies += [*direct[h], *later[h]]
        first = later
    for h in range(2):
        for cp in first[h]:
            cp.wait_recv()
    for cp in copies:
        cp.wait_send()


def gather_weights(shard):
    out = pl.pallas_call(
        gather_kernel,
        out_shape=jax.ShapeDtypeStruct((2, 4, 4, PADDED, 640), jnp.bfloat16),
        in_specs=vmem_specs(1),
        out_specs=vmem_specs(1)[0],
        scratch_shapes=[pltpu.SemaphoreType.DMA((18,)), pltpu.SemaphoreType.DMA((18,))],
        compiler_params=params(0),
        name="gather_weights",
    )(shard)
    return out.reshape(32 * PADDED, 640)


def f32(v):
    return v.astype(jnp.float32)


def bf(v):
    return v.astype(jnp.bfloat16)


def copier(send, recv):
    def copy(n, src, dst, to):
        cp = pltpu.make_async_remote_copy(
            src_ref=src, dst_ref=dst, send_sem=send.at[n], recv_sem=recv.at[n],
            device_id=to, device_id_type=MESH,
        )
        cp.start()
        return cp

    return copy


def take_turns(*parts):
    running = list(parts)
    while running:
        for part in list(running):
            try:
                next(part)
            except StopIteration:
                running.remove(part)


def scatter_steps(t_ref, out_ref, far, near, stage, acc1, far2, near2, stage2, acc2, last, send, recv):
    c, z, y, x = place()
    e = lax.axis_index(EXP)
    copy = copier(send, recv)

    def dev(zz, yy, xx):
        return (zz * 16 + ((yy + 4) % 4) * 4 + (xx + 4) % 4, e)

    rows = (pl.ds(0, 48), pl.ds(48, 48))
    copies = []

    def ring(along_x):
        me = x if along_x else y
        up = dev(z, y, x + 1) if along_x else dev(z, y + 1, x)
        down = dev(z, y, x - 1) if along_x else dev(z, y - 1, x)
        return me, (me + 3) % 4, (me + 1) % 4, (me + 2) % 4, up, down

    def first_source(h, zsel, pos):
        return t_ref.at[zsel, pos, :, rows[h]] if h == 0 else t_ref.at[zsel, :, pos, rows[h]]

    def second_source(h, zsel, pos):
        return acc1.at[h, zsel, pos]

    final = []
    for phase, source, far_ref, near_ref, stage_ref, acc in (
        (1, first_source, far, near, stage, acc1),
        (2, second_source, far2, near2, stage2, acc2),
    ):
        started = []
        for h in range(2):
            me, low, high, across, up, down = ring((h == 1) == (phase == 1))
            n = (phase - 1) * 12 + h * 6
            started.append([
                copy(n, source(h, 0, across), far_ref.at[h, 0], up),
                copy(n + 1, source(h, 1, across), far_ref.at[h, 1], down),
                copy(n + 2, source(h, 1, high), near_ref.at[h, 0, 1], up),
                copy(n + 3, source(h, 0, low), near_ref.at[h, 1, 0], down),
            ])
        yield
        for h in range(2):
            me, low, high, across, up, down = ring((h == 1) == (phase == 1))
            n = (phase - 1) * 12 + h * 6
            started[h][0].wait_recv()
            stage_ref[h, 0] = bf(f32(source(h, 0, high)[...]) + f32(far_ref[h, 0]))
            started[h].append(copy(n + 4, stage_ref.at[h, 0], near_ref.at[h, 0, 0], up))
            started[h][1].wait_recv()
            stage_ref[h, 1] = bf(f32(source(h, 1, low)[...]) + f32(far_ref[h, 1]))
            started[h].append(copy(n + 5, stage_ref.at[h, 1], near_ref.at[h, 1, 1], down))
        yield
        for h in range(2):
            me = ring((h == 1) == (phase == 1))[0]
            for i in (2, 3, 4, 5):
                started[h][i].wait_recv()
            for zz in range(2):
                acc[h, zz] = bf(
                    f32(source(h, zz, me)[...]) + f32(near_ref[h, 0, zz]) + f32(near_ref[h, 1, zz])
                )
            copies += started[h]
            if phase == 2:
                final.append(copy(24 + h, acc2.at[h, 1 - z], last.at[h], dev(1 - z, y, x)))
    yield
    for h in range(2):
        final[h].wait_recv()
        out_ref[rows[h], :] = bf(f32(acc2[h, z]) + f32(last[h]))
    for cp in copies + final:
        cp.wait_send()


def scatter_scratch():
    b = jnp.bfloat16
    return [
        pltpu.VMEM((2, 2, 4, 48, 640), b),
        pltpu.VMEM((2, 2, 2, 4, 48, 640), b),
        pltpu.VMEM((2, 2, 4, 48, 640), b),
        pltpu.VMEM((2, 2, 4, 48, 640), b),
        pltpu.VMEM((2, 2, 48, 640), b),
        pltpu.VMEM((2, 2, 2, 48, 640), b),
        pltpu.VMEM((2, 2, 48, 640), b),
        pltpu.VMEM((2, 2, 48, 640), b),
        pltpu.VMEM((2, 48, 640), b),
        pltpu.SemaphoreType.DMA((26,)),
        pltpu.SemaphoreType.DMA((26,)),
    ]


def exp_peers():
    c = lax.axis_index(CTX)
    e = lax.axis_index(EXP)
    h, k = e // 2, e % 2
    return (c, e + 1 - 2 * k), (c, ((h + 1) % 4) * 2 + k), (c, ((h + 3) % 4) * 2 + k)


def sum_steps(post, part, out, mate, stage, far, near, send, recv):
    e = lax.axis_index(EXP)
    h, k = e // 2, e % 2
    partner, up, down = exp_peers()
    copy = copier(send, recv)
    lanes = (pl.ds(0, 1408), pl.ds(1408, MODEL - 1408))

    def rows(core, block):
        return pl.ds(pl.multiple_of(core * 64 + block * 16, 16), 16)

    high, low, across = (h + 1) % 4, (h + 3) % 4, (h + 2) % 4
    order = (across, high, low, h)
    pair = [copy(i, part.at[rows(1 - k, b)], mate.at[b], partner) for i, b in enumerate(order)]
    yield
    pair[0].wait_recv()
    stage[across] = bf(f32(part[rows(k, across), :]) + f32(mate[across]))
    copies = [
        copy(4, stage.at[across, :, lanes[0]], far.at[:, lanes[0]], up),
        copy(5, stage.at[across, :, lanes[1]], far.at[:, lanes[1]], down),
    ]
    pair[1].wait_recv()
    stage[high] = bf(f32(part[rows(k, high), :]) + f32(mate[high]))
    copies.append(copy(6, stage.at[high, :, lanes[1]], near.at[0, :, lanes[1]], up))
    pair[2].wait_recv()
    stage[low] = bf(f32(part[rows(k, low), :]) + f32(mate[low]))
    copies.append(copy(7, stage.at[low, :, lanes[0]], near.at[1, :, lanes[0]], down))
    yield
    copies[0].wait_recv()
    stage[high, :, lanes[0]] = bf(f32(stage[high, :, lanes[0]]) + f32(far[:, lanes[0]]))
    copies.append(copy(8, stage.at[high, :, lanes[0]], near.at[0, :, lanes[0]], up))
    copies[1].wait_recv()
    stage[low, :, lanes[1]] = bf(f32(stage[low, :, lanes[1]]) + f32(far[:, lanes[1]]))
    copies.append(copy(9, stage.at[low, :, lanes[1]], near.at[1, :, lanes[1]], down))
    pair[3].wait_recv()
    total = f32(part[rows(k, h), :]) + f32(mate[h])
    yield
    for cp in copies[2:]:
        cp.wait_recv()
    mine = rows(k, h)
    out[mine, :] = post(total + f32(near[0]) + f32(near[1]), mine)
    direct = [copy(10, out.at[mine], out.at[mine], up), copy(11, out.at[mine], out.at[mine], down)]
    passed = [copy(12, out.at[mine], out.at[mine], partner)]
    yield
    theirs = rows(k, low), rows(k, high)
    for i, to in enumerate((up, down)):
        direct[i].wait_recv()
        view = out.at[theirs[i], lanes[i]]
        direct.append(copy(13 + i, view, view, to))
    for i in range(2):
        passed.append(copy(15 + i, out.at[theirs[i]], out.at[theirs[i]], partner))
    yield
    for i in range(2):
        direct[2 + i].wait_recv()
        view = out.at[rows(k, across), lanes[i]]
        passed.append(copy(17 + i, view, view, partner))
    yield
    for cp in passed:
        cp.wait_recv()
    for cp in [*pair, *copies, *direct, *passed]:
        cp.wait_send()


def sum_scratch():
    b = jnp.bfloat16
    return [
        pltpu.VMEM((4, 16, MODEL), b),
        pltpu.VMEM((4, 16, MODEL), b),
        pltpu.VMEM((16, MODEL), b),
        pltpu.VMEM((2, 16, MODEL), b),
        pltpu.SemaphoreType.DMA((20,)),
        pltpu.SemaphoreType.DMA((20,)),
    ]


def ring_ctx():
    c = lax.axis_index(CTX)
    e = lax.axis_index(EXP)
    return ((c + 1) % 32, e), ((c + 31) % 32, e)


def drop_into(ref, values):
    for i in range(32):
        ref[:, SHARD * i : SHARD * (i + 1)] = values[:, PADDED * i : PADDED * i + SHARD]


def attention_kernel(
    normed_pad, full, tokens, residual, projected, span, attended, prob_ref, part, rim_send, rim_recv, *scratch
):
    c = lax.axis_index(CTX)
    after, before = ring_ctx()
    greet([*exp_peers(), after, before])
    made = bf(dot(normed_pad[...], full[:, :384]))
    projected[...] = made
    span[128:, :] = made[:, 256:]
    rim = copier(rim_send, rim_recv)(0, span.at[pl.ds(128, 128)], span.at[pl.ds(0, 128)], after)
    query_pos, key_pos = iota((128, 256), 0), iota((128, 256), 1)
    valid = (key_pos <= query_pos + 128) & (key_pos > query_pos) & (key_pos + c * 128 >= 128)
    rim.wait_recv()
    keys, values = span[:, :HEAD_SIZE], span[:, HEAD_SIZE:]
    for h in range(GROUP):
        scores = dot_nt(made[:, HEAD_SIZE * h : HEAD_SIZE * (h + 1)], keys) * 0.125
        weights = jnp.where(valid, jnp.exp(scores), 0.0)
        prob = weights / jnp.sum(weights, axis=-1, keepdims=True)
        prob_ref[h] = prob
        attended[:, HEAD_SIZE * h : HEAD_SIZE * (h + 1)] = bf(dot(bf(prob), values))
    drop_into(part, bf(dot_nt(attended[...], full[:, 384:])))
    rim.wait_send()
    take_turns(sum_steps(lambda t, m: add_base(t, m, tokens), part, residual, *scratch))


def attention(normed_pad, full, tokens):
    b = jnp.bfloat16
    shape = jax.ShapeDtypeStruct
    return pl.pallas_call(
        attention_kernel,
        out_shape=[
            shape((128, MODEL), b), shape((128, 384), b), shape((256, 128), b), shape((128, 256), b),
            shape((4, 128, 256), jnp.float32),
        ],
        in_specs=vmem_specs(3),
        out_specs=vmem_specs(5),
        scratch_shapes=[
            pltpu.VMEM((128, MODEL), b), pltpu.SemaphoreType.DMA((1,)), pltpu.SemaphoreType.DMA((1,)),
        ] + sum_scratch(),
        compiler_params=params(1),
        name="attention",
    )(normed_pad, full, tokens)


def grad_residual_kernel(part, cotangent, residual, out, own, *scratch):
    greet(exp_peers())
    take_turns(sum_steps(lambda t, m: finish_resid(t, m, cotangent, residual, own), part, out, *scratch))


def grad_residual(part, cotangent, residual):
    return pl.pallas_call(
        grad_residual_kernel,
        out_shape=[
            jax.ShapeDtypeStruct((128, MODEL), jnp.bfloat16),
            jax.ShapeDtypeStruct((16, MODEL), jnp.float32),
        ],
        in_specs=vmem_specs(3),
        out_specs=vmem_specs(2),
        scratch_shapes=sum_scratch(),
        compiler_params=params(3),
        name="grad_residual",
    )(part, cotangent, residual)


def last_kernel(
    moe_part, residual, tokens, grad_resid, grad_resid_bf, normed_pad, full, projected, span, attended, prob_ref,
    block_out, grad_tokens, sums,
    resid_pad, qkv_grad, rim_out, rim_in, grad_part, terms, rim_send, rim_recv, *scratch
):
    c, z, y, x = place()
    e = lax.axis_index(EXP)
    after, before = ring_ctx()
    near = [
        ((1 - z) * 16 + y * 4 + x, e),
        (z * 16 + (y + 1) % 4 * 4 + x, e),
        (z * 16 + (y + 3) % 4 * 4 + x, e),
        (z * 16 + y * 4 + (x + 1) % 4, e),
        (z * 16 + y * 4 + (x + 3) % 4, e),
    ]
    greet([*near, *exp_peers(), after, before])
    block_sum = sum_steps(lambda t, m: add_base(t, m, residual), moe_part, block_out, *scratch[6:12])
    next(block_sum)

    resid_pad[...] = jnp.zeros_like(resid_pad)
    for i in range(32):
        resid_pad[:, PADDED * i : PADDED * i + SHARD] = grad_resid_bf[:, SHARD * i : SHARD * (i + 1)]
    attended_grad = bf(dot(resid_pad[...], full[:, 384:]))
    keys, values = span[:, :HEAD_SIZE], span[:, HEAD_SIZE:]
    grad_key = jnp.zeros((256, HEAD_SIZE), jnp.float32)
    grad_value = jnp.zeros((256, HEAD_SIZE), jnp.float32)
    for h in range(GROUP):
        head = pl.ds(HEAD_SIZE * h, HEAD_SIZE)
        grad_out = attended_grad[:, HEAD_SIZE * h : HEAD_SIZE * (h + 1)]
        prob = prob_ref[h]
        grad_prob = dot_nt(grad_out, values)
        grad_value = grad_value + dot_tn(bf(prob), grad_out)
        inner = jnp.sum(grad_prob * prob, axis=-1, keepdims=True)
        grad_score = bf(prob * (grad_prob - inner) * 0.125)
        qkv_grad[:, head] = bf(dot(grad_score, keys))
        grad_key = grad_key + dot_tn(grad_score, projected[:, head])
    rim_out[:, :HEAD_SIZE] = bf(grad_key[:128])
    rim_out[:, HEAD_SIZE:] = bf(grad_value[:128])
    rim = copier(rim_send, rim_recv)(0, rim_out, rim_in, before)

    def term(left, right, columns):
        def four(i, t):
            rows = left[:, pl.ds(pl.multiple_of(i * 384, 128), 384)]
            terms[i // 4, i % 4, :, :, columns] = bf(dot_tn(rows, right)).reshape(4, PADDED, columns.size)
            return t

        lax.fori_loop(0, 8, four, 0)

    term(resid_pad, attended[...], pl.ds(384, 256))
    next(block_sum)
    rim.wait()
    qkv_grad[:, 256:320] = bf(grad_key[128:] + f32(rim_in[:, :HEAD_SIZE]))
    qkv_grad[:, 320:] = bf(grad_value[128:] + f32(rim_in[:, HEAD_SIZE:]))
    grads = qkv_grad[...]
    drop_into(grad_part, bf(dot_nt(grads, full[:, :384])))
    token_sum = sum_steps(
        lambda t, m: finish_tokens(t, m, tokens, grad_resid), grad_part, grad_tokens, *scratch[:6]
    )
    next(token_sum)
    term(normed_pad, grads, pl.ds(0, 384))
    take_turns(scatter_steps(terms, sums, *scratch[12:]), token_sum, block_sum)


def last_sums(*operands):
    b = jnp.bfloat16
    return pl.pallas_call(
        last_kernel,
        out_shape=[
            jax.ShapeDtypeStruct((128, MODEL), b), jax.ShapeDtypeStruct((128, MODEL), b),
            jax.ShapeDtypeStruct((PADDED, 640), b),
        ],
        in_specs=vmem_specs(11),
        out_specs=vmem_specs(3),
        scratch_shapes=[
            pltpu.VMEM((128, 32 * PADDED), b),
            pltpu.VMEM((128, 384), b),
            pltpu.VMEM((128, 128), b),
            pltpu.VMEM((128, 128), b),
            pltpu.VMEM((128, MODEL), b),
            pltpu.VMEM((2, 4, 4, PADDED, 640), b),
            pltpu.SemaphoreType.DMA((1,)),
            pltpu.SemaphoreType.DMA((1,)),
        ] + sum_scratch() + sum_scratch() + scatter_scratch(),
        compiler_params=params(4),
        name="last_sums",
    )(*operands)


EPSILON = 1e-05
GLU_ALPHA = 1.702
QUERY_HEADS = 32
KEY_VALUE_HEADS = 8
HEAD_SIZE = 64
WINDOW = 128
MODEL = 2880
GROUP = QUERY_HEADS // KEY_VALUE_HEADS


def dot(a, b):
    return jnp.dot(a, b, preferred_element_type=jnp.float32)


def dot_tn(a, b):
    return lax.dot_general(a, b, (((0,), (0,)), ((), ())), preferred_element_type=jnp.float32)


def dot_nt(a, b):
    return lax.dot_general(a, b, (((1,), (1,)), ((), ())), preferred_element_type=jnp.float32)


def inverse_rms(values):
    return lax.rsqrt(jnp.mean(values * values, axis=-1, keepdims=True) + EPSILON)


def rms_back(values, inv_rms, grad_in):
    inner_mean = jnp.mean(grad_in * values, axis=-1, keepdims=True)
    return inv_rms * grad_in - values * (inv_rms * inv_rms * inv_rms) * inner_mean


def pad_features(v):
    return jnp.pad(v.reshape(-1, 32, SHARD), ((0, 0), (0, 0), (0, PADDED - SHARD))).reshape(-1, 32 * PADDED)


def iota(shape, axis):
    return lax.broadcasted_iota(jnp.int32, shape, axis)


def spread_extra(q):
    r, j = iota((128, 512), 0), iota((128, 512), 1)
    return bf((j == (r // 4) * 16 + q * 4 + r % 4).astype(jnp.float32))


def expert_kernel(
    x_ref, cot_ref, ids_ref, combine_ref, wg, wu, wd,
    grad_in_part, moe_part, grad_gate, grad_up, grad_down,
    xp, one_hot, extra_hot, weight_ref, scale, send_buf, got, ext, gate_pre, up_pre, act, gg, gu, parts, other, back,
    send, recv, send2, recv2, send3, recv3, send4, recv4,
):
    c = lax.axis_index(CTX)
    e = lax.axis_index(EXP)
    k = e % 2
    partner = (c, e + 1 - 2 * k)
    group, inner = c // 8, c % 8
    barrier = pltpu.get_barrier_semaphore()

    def moved(n, sign):
        return ((group + sign * (n // 8) + 4) % 4) * 8 + (inner + sign * (n % 8) + 8) % 8

    def hello(n, t):
        pl.semaphore_signal(barrier, inc=1, device_id=(moved(n, 1), e), device_id_type=MESH)
        return t

    lax.fori_loop(1, 32, hello, 0)
    pl.semaphore_signal(barrier, inc=1, device_id=partner, device_id_type=MESH)

    lane = iota((128, 512), 1)
    hot = jnp.zeros((128, 512), jnp.float32)
    weight = jnp.zeros((128, 512), jnp.float32)
    for route in range(4):
        match = ids_ref[:, route : route + 1] == lane // 16
        hot = jnp.where(match, 1.0, hot)
        weight = jnp.where(match, combine_ref[:, route : route + 1], weight)
    weight_ref[...] = weight
    below = bf(jnp.where(iota((128, 128), 0) > iota((128, 128), 1), 1.0, 0.0))
    slot = jnp.where(hot > 0, dot(below, bf(hot)), 64.0)
    main = slot == f32(lane % 16)
    extra = slot == f32(16 + lane % 4)
    one_hot[...] = bf(jnp.where(main, 1.0, 0.0))
    for q in range(4):
        extra_hot[q] = bf(jnp.where(extra & (lane % 16 // 4 == q), 1.0, 0.0))
    scale[0] = jnp.sum(jnp.where(main, weight, 0.0).T, axis=1, keepdims=True)
    scale[1] = jnp.sum(jnp.where(extra, weight, 0.0).T, axis=1, keepdims=True)
    res = f32(x_ref[...])
    for a, rows in enumerate((bf(res * inverse_rms(res)), cot_ref[...])):
        xp[a, :, :MODEL] = rows
        xp[a, :, MODEL:] = jnp.zeros((128, 192), jnp.bfloat16)

    def out_copy(a, n):
        to = moved(n, 1)
        return pltpu.make_async_remote_copy(
            src_ref=send_buf.at[a, to], dst_ref=got.at[a, k, c],
            send_sem=send.at[a, n], recv_sem=recv.at[a, n],
            device_id=(to, e), device_id_type=MESH,
        )

    def over(a, n):
        source = moved(n, -1)
        return pltpu.make_async_remote_copy(
            src_ref=got.at[a, k, source], dst_ref=got.at[a, k, source],
            send_sem=send2.at[a, n], recv_sem=recv2.at[a, n],
            device_id=partner, device_id_type=MESH,
        )

    def pack(a, j, t):
        g = (group + j) % 4
        at = pl.ds(pl.multiple_of(g * 128, 128), 128)
        dest = pl.ds(g * 8, 8)
        m = one_hot[:, at]
        s0 = scale[0, at, :] if a else 1.0
        s1 = scale[1, at, :] if a else 1.0

        @pl.when(k == 0)
        def _():
            low = dot_tn(m, xp[a, :, :HALF_LANES])
            send_buf[a, dest] = bf(low * s0 if a else low).reshape(8, 16, HALF_LANES)

        @pl.when(k == 1)
        def _():
            high = dot_tn(m, xp[a, :, HALF_LANES:2944])
            send_buf[a, dest, :, 0:1024] = bf(high * s0 if a else high).reshape(8, 16, 1024)
            quarters = dot_tn(extra_hot[0, :, at], xp[a, :, 0:768])
            for q in range(1, 4):
                quarters = quarters + dot_tn(extra_hot[q, :, at], xp[a, :, 768 * q : 768 * q + 768])
            send_buf[a, dest, :, 1024:1792] = bf(quarters * s1 if a else quarters).reshape(8, 16, 768)
            send_buf[a, dest, :, 1792:] = jnp.zeros((8, 16, 128), jnp.bfloat16)

        return t

    def start_group(a, j):
        first = 1 if j == 0 else 0
        lax.fori_loop(first, 8, lambda i, t: (out_copy(a, j * 8 + i).start(), t)[1], 0)

    for a in range(2):
        for j in range(4):
            pack(a, j, 0)
            if a == 0 and j == 0:
                pl.semaphore_wait(barrier, 32)
            start_group(a, j)
        got[a, k, c] = send_buf[a, c]
        over(a, 0).start()

    def arrived(a, n, t):
        out_copy(a, n).wait_recv()
        over(a, n).start()
        return t

    def take(a):
        lax.fori_loop(1, 32, lambda n, t: arrived(a, n, t), 0)
        lax.fori_loop(0, 32, lambda n, t: (over(a, n).wait(), t)[1], 0)
        packed = got[a, 1, :, :, 1024:1792].reshape(512, 768)
        for q in range(4):
            ext[a, :, 768 * q : 768 * q + 768] = bf(dot(spread_extra(q), packed))

    def rows_of(a, t):
        first = got[a, 0, pl.ds(t * 16, 16)].reshape(256, HALF_LANES)
        second = got[a, 1, pl.ds(t * 16, 16), :, 0:960].reshape(256, 960)
        return first, second

    def at_rows(t):
        return pl.ds(pl.multiple_of(t * 256, 256), 256)

    take(0)

    def forward(t, carry):
        first, second = rows_of(0, t)
        for w, into in ((wg, gate_pre), (wu, up_pre)):
            into[at_rows(t), :] = dot(first, w[:HALF_LANES]) + dot(second, w[HALF_LANES:])
        return carry

    lax.fori_loop(0, 2, forward, 0)
    for w, into in ((wg, gate_pre), (wu, up_pre)):
        into[512:, :] = dot(ext[0, :, :MODEL], w[...])

    take(1)

    def pointwise(rows, grad_act):
        gate, up = gate_pre[rows, :], up_pre[rows, :] + 1.0
        sig = jax.nn.sigmoid(GLU_ALPHA * gate)
        glu = gate * sig
        act[rows, :] = bf(glu * up)
        gg[rows, :] = bf(grad_act * up * (sig + GLU_ALPHA * glu * (1.0 - sig)))
        gu[rows, :] = bf(grad_act * glu)

    def backward(t, carry):
        first, second = rows_of(1, t)
        pointwise(at_rows(t), dot_nt(first, wd[:, :HALF_LANES]) + dot_nt(second, wd[:, HALF_LANES:]))
        return carry

    lax.fori_loop(0, 2, backward, 0)
    pointwise(pl.ds(512, 128), dot_nt(ext[1, :, :MODEL], wd[...]))

    for a in range(2):
        lax.fori_loop(1, 32, lambda n, t, a=a: (out_copy(a, n).wait_send(), t)[1], 0)

    def across(a, j):
        block = pl.ds(((group + j) % 4) * 8, 8)
        return pltpu.make_async_remote_copy(
            src_ref=parts.at[a, 1 - k, block], dst_ref=other.at[a, block],
            send_sem=send3.at[a, j], recv_sem=recv3.at[a, j],
            device_id=partner, device_id_type=MESH,
        )

    def home(a, n):
        to = moved(n, 1)
        return pltpu.make_async_remote_copy(
            src_ref=send_buf.at[a, to], dst_ref=back.at[a, c],
            send_sem=send4.at[a, n], recv_sem=recv4.at[a, n],
            device_id=(to, e), device_id_type=MESH,
        )

    def result(a, rows):
        if a == 0:
            return bf(dot_nt(gg[rows, :], wg[...]) + dot_nt(gu[rows, :], wu[...]))
        return bf(dot(act[rows, :], wd[...]))

    def add_pair(a, j):
        across(a, j).wait_recv()

        def one(i, t):
            n = j * 8 + i
            to = moved(n, 1)
            send_buf[a, to] = bf(f32(parts[a, k, to]) + f32(other[a, to]))

            @pl.when(n > 0)
            def _():
                home(a, n).start()

            return t

        lax.fori_loop(0, 8, one, 0)
        if j == 0:
            back[a, c] = send_buf[a, c]

    steps = [(a, j) for a in range(2) for j in range(4)]
    for index, (a, j) in enumerate(steps):
        if j == 0:
            last = result(a, pl.ds(512, 128))
            folded = jnp.zeros((512, 768), jnp.float32)
            for q in range(4):
                width = 768 if q < 3 else 576
                piece = dot_tn(spread_extra(q), last[:, 768 * q : 768 * q + width])
                if q == 3:
                    piece = jnp.concatenate([piece, jnp.zeros((512, 192), jnp.float32)], axis=1)
                folded = folded + piece
            parts[a, 1, :, :, 1024:1792] = bf(folded).reshape(32, 16, 768)
            parts[a, 1, :, :, 960:1024] = jnp.zeros((32, 16, 64), jnp.bfloat16)
            parts[a, 1, :, :, 1792:] = jnp.zeros((32, 16, 128), jnp.bfloat16)
        g = (group + j) % 4
        rows = result(a, pl.ds(pl.multiple_of(g * 128, 128), 128))
        parts[a, 0, pl.ds(g * 8, 8)] = rows[:, :HALF_LANES].reshape(8, 16, HALF_LANES)
        parts[a, 1, pl.ds(g * 8, 8), :, 0:960] = rows[:, HALF_LANES:].reshape(8, 16, 960)
        across(a, j).start()
        if index:
            add_pair(*steps[index - 1])
    add_pair(*steps[-1])

    def grads_at(columns, lanes, half):
        x_main = got[0, half, :, :, lanes].reshape(512, lanes.size)
        g_main = got[1, half, :, :, lanes].reshape(512, lanes.size)
        x_ext, g_ext = ext[0, :, columns], ext[1, :, columns]
        grad_gate[columns, :] = bf(dot_tn(x_main, gg[:512, :]) + dot_tn(x_ext, gg[512:, :]))
        grad_up[columns, :] = bf(dot_tn(x_main, gu[:512, :]) + dot_tn(x_ext, gu[512:, :]))
        grad_down[:, columns] = bf(dot_tn(act[:512, :], g_main) + dot_tn(act[512:, :], g_ext))

    def lower(i, t):
        lanes = pl.ds(pl.multiple_of(i * 384, 128), 384)
        grads_at(lanes, lanes, 0)
        return t

    lax.fori_loop(0, 5, lower, 0)
    grads_at(pl.ds(1920, 512), pl.ds(0, 512), 1)
    grads_at(pl.ds(2432, 448), pl.ds(512, 448), 1)

    for a, into in enumerate((grad_in_part, moe_part)):
        lax.fori_loop(1, 32, lambda n, t, a=a: (home(a, n).wait_recv(), t)[1], 0)

        def summed(hot, lanes, a=a):
            rows = back[a, :, :, lanes].reshape(512, lanes.size)
            if a == 0:
                return dot(hot, rows)
            spread = jnp.where(hot > 0, weight_ref[...], 0.0)
            high = bf(spread)
            return dot(high, rows) + dot(bf(spread - f32(high)), rows)

        @pl.when(k == 0)
        def _(into=into, summed=summed):
            into[:, :HALF_LANES] = bf(summed(one_hot[...], pl.ds(0, HALF_LANES)))
            into[:, HALF_LANES:] = jnp.zeros((128, 960), jnp.bfloat16)

        @pl.when(k == 1)
        def _(into=into, summed=summed):
            upper = summed(one_hot[...], pl.ds(0, 1024))
            quarters = [summed(extra_hot[q], pl.ds(1024, 768)) for q in range(4)]
            into[:, 0:768] = bf(quarters[0])
            into[:, 768:1536] = bf(quarters[1])
            into[:, 1536:1920] = bf(quarters[2][:, :384])
            into[:, 1920:2304] = bf(quarters[2][:, 384:] + upper[:, :384])
            into[:, 2304:] = bf(quarters[3][:, :576] + upper[:, 384:960])

    for a in range(2):
        lax.fori_loop(1, 32, lambda n, t, a=a: (home(a, n).wait_send(), t)[1], 0)
        lax.fori_loop(0, 4, lambda j, t, a=a: (across(a, j).wait_send(), t)[1], 0)


def experts(residual, cotangent, expert_ids, combine_weights, w_gate, w_up, w_down):
    b = jnp.bfloat16
    shape = jax.ShapeDtypeStruct
    return pl.pallas_call(
        expert_kernel,
        out_shape=[
            shape((128, MODEL), b), shape((128, MODEL), b),
            shape((MODEL, 256), b), shape((MODEL, 256), b), shape((256, MODEL), b),
        ],
        in_specs=vmem_specs(7),
        out_specs=vmem_specs(5),
        scratch_shapes=[
            pltpu.VMEM((2, 128, 3072), b),
            pltpu.VMEM((128, 512), b),
            pltpu.VMEM((4, 128, 512), b),
            pltpu.VMEM((128, 512), jnp.float32),
            pltpu.VMEM((2, 512, 1), jnp.float32),
            pltpu.VMEM((2, 32, 16, HALF_LANES), b),
            pltpu.VMEM((2, 2, 32, 16, HALF_LANES), b),
            pltpu.VMEM((2, 128, 3072), b),
            pltpu.VMEM((640, 256), jnp.float32),
            pltpu.VMEM((640, 256), jnp.float32),
            pltpu.VMEM((640, 256), b),
            pltpu.VMEM((640, 256), b),
            pltpu.VMEM((640, 256), b),
            pltpu.VMEM((2, 2, 32, 16, HALF_LANES), b),
            pltpu.VMEM((2, 32, 16, HALF_LANES), b),
            pltpu.VMEM((2, 32, 16, HALF_LANES), b),
        ] + [pltpu.SemaphoreType.DMA((2, 32))] * 4
        + [pltpu.SemaphoreType.DMA((2, 4))] * 2 + [pltpu.SemaphoreType.DMA((2, 32))] * 2,
        compiler_params=params(2),
        name="experts",
    )(residual, cotangent, expert_ids, combine_weights, w_gate, w_up, w_down)


def add_base(total, mine, base):
    return bf(f32(base[mine, :]) + total)


def finish_resid(total, mine, cot, resid, grad_resid):
    values = f32(resid[mine, :])
    out = f32(cot[mine, :]) + rms_back(values, inverse_rms(values), total)
    grad_resid[...] = out
    return bf(out)


def finish_tokens(total, mine, tokens, grad_resid):
    values = f32(tokens[mine, :])
    return bf(grad_resid[...] + rms_back(values, inverse_rms(values), total))


def body(
    tokens, cotangent, expert_ids, combine_weights,
    w_query, key_value_weight, w_output, w_gate, w_up, w_down,
):
    tokens_f32 = f32(tokens)
    normed = bf(tokens_f32 * inverse_rms(tokens_f32))
    normed_pad = pad_features(normed)
    shard = jnp.concatenate([w_query, key_value_weight, w_output.T], axis=1)
    full = gather_weights(jnp.pad(shard, ((0, PADDED - SHARD), (0, 0))))

    residual, projected, span, attended, prob = attention(normed_pad, full, tokens)
    grad_in_part, moe_part, grad_gate, grad_up, grad_down = experts(
        residual, cotangent, expert_ids, combine_weights, w_gate[0], w_up[0], w_down[0]
    )
    grad_resid_bf, grad_resid = grad_residual(grad_in_part, cotangent, residual)
    block_out, grad_tokens, sums = last_sums(
        moe_part, residual, tokens, grad_resid, grad_resid_bf, normed_pad, full, projected, span, attended, prob
    )
    sums = sums[:SHARD]
    return (
        block_out, grad_tokens, sums[:, :256], sums[:, 256:384], sums[:, 384:].T,
        grad_gate[None], grad_up[None], grad_down[None],
    )


def solution(mesh):
    in_specs = (
        P("ctx", None), P("ctx", None), P("ctx", None), P("ctx", None),
        P("ctx", "exp"), P("ctx", "exp"), P("exp", "ctx"),
        P("ctx", None, "exp"), P("ctx", None, "exp"), P("ctx", "exp", None),
    )
    out_specs = (
        P("ctx", None), P("ctx", None), P("ctx", "exp"), P("ctx", "exp"), P("exp", "ctx"),
        P("ctx", None, "exp"), P("ctx", None, "exp"), P("ctx", "exp", None),
    )
    return jax.shard_map(body, mesh=mesh, in_specs=in_specs, out_specs=out_specs, check_vma=False)
```

```python
import functools

import jax
import jax.numpy as jnp
from jax import lax
from jax.experimental import pallas as pl
from jax.experimental.pallas import tpu as pltpu
from jax.sharding import PartitionSpec as P

CTX, EXP = "ctx", "exp"
SHARD = 90
PADDED = 96
HALF_LANES = 1920
MESH = pl.DeviceIdType.MESH
VMEM_BYTES = 60 * 2**20


def params(collective_id):
    return pltpu.CompilerParams(
        collective_id=collective_id, has_side_effects=True, vmem_limit_bytes=VMEM_BYTES
    )


def vmem_specs(count):
    return [pl.BlockSpec(memory_space=pltpu.VMEM)] * count


def place():
    c = lax.axis_index(CTX)
    return c, c // 16, (c // 4) % 4, c % 4


def greet(peers):
    barrier = pltpu.get_barrier_semaphore()
    for peer in peers:
        pl.semaphore_signal(barrier, inc=1, device_id=peer, device_id_type=MESH)
    pl.semaphore_wait(barrier, len(peers))


def gather_steps(w_ref, out_ref, send, recv):
    c, z, y, x = place()
    e = lax.axis_index(EXP)
    copy = copier(send, recv)

    def dev(zz, yy, xx):
        return (zz * 16 + ((yy + 4) % 4) * 4 + (xx + 4) % 4, e)

    rows = (pl.ds(0, 48), pl.ds(48, 48))
    copies = []
    first = []
    for h in range(2):
        first.append(copy(h, w_ref.at[rows[h]], out_ref.at[z, y, x, rows[h]], dev(1 - z, y, x)))
    out_ref[z, y, x] = w_ref[...]
    copies += first

    def view(h, phase, zsel, pos):
        along_x = (h == 0) == (phase == 1)
        if phase == 1:
            return out_ref.at[zsel, y, pos, rows[h]] if along_x else out_ref.at[zsel, pos, x, rows[h]]
        return out_ref.at[zsel, :, pos, rows[h]] if along_x else out_ref.at[zsel, pos, :, rows[h]]

    def ring(h, phase):
        along_x = (h == 0) == (phase == 1)
        me = x if along_x else y
        up = dev(z, y, x + 1) if along_x else dev(z, y + 1, x)
        down = dev(z, y, x - 1) if along_x else dev(z, y - 1, x)
        return me, (me + 3) % 4, (me + 1) % 4, up, down

    yield
    for phase in (1, 2):
        direct = []
        for h in range(2):
            for cp in first[h] if phase == 2 else (first[h],):
                cp.wait_recv()
            me, low, high, up, down = ring(h, phase)
            n = 2 + (phase - 1) * 8 + h * 4
            both = pl.ds(0, 2)
            direct.append((
                copy(n, view(h, phase, both, me), view(h, phase, both, me), up),
                copy(n + 1, view(h, phase, both, me), view(h, phase, both, me), down),
            ))
        yield
        later = []
        for h in range(2):
            me, low, high, up, down = ring(h, phase)
            n = 2 + (phase - 1) * 8 + h * 4
            direct[h][0].wait_recv()
            a = copy(n + 2, view(h, phase, 0, low), view(h, phase, 0, low), up)
            direct[h][1].wait_recv()
            b = copy(n + 3, view(h, phase, 1, high), view(h, phase, 1, high), down)
            later.append((a, b))
        for h in range(2):
            copies += [*direct[h], *later[h]]
        first = later
        yield
    for h in range(2):
        for cp in first[h]:
            cp.wait_recv()
    for cp in copies:
        cp.wait_send()


def near_peers():
    c, z, y, x = place()
    e = lax.axis_index(EXP)
    return [
        ((1 - z) * 16 + y * 4 + x, e),
        (z * 16 + (y + 1) % 4 * 4 + x, e),
        (z * 16 + (y + 3) % 4 * 4 + x, e),
        (z * 16 + y * 4 + (x + 1) % 4, e),
        (z * 16 + y * 4 + (x + 3) % 4, e),
    ]


def pad_into(ref, values):
    ref[...] = jnp.zeros_like(ref)
    for i in range(32):
        ref[:, PADDED * i : PADDED * i + SHARD] = values[:, SHARD * i : SHARD * (i + 1)]


def gather_kernel(qkv_ref, o_ref, tokens, full_qkv, full_o, normed_pad, s0, r0, s1, r1):
    greet(near_peers())
    first, second = gather_steps(qkv_ref, full_qkv, s0, r0), gather_steps(o_ref, full_o, s1, r1)
    next(first)
    next(second)
    values = f32(tokens[...])
    pad_into(normed_pad, bf(values * inverse_rms(values)))
    take_turns(first, second)


def gather_weights(qkv, out, tokens):
    b = jnp.bfloat16
    full_qkv, full_o, normed_pad = pl.pallas_call(
        gather_kernel,
        out_shape=[
            jax.ShapeDtypeStruct((2, 4, 4, PADDED, 384), b),
            jax.ShapeDtypeStruct((2, 4, 4, PADDED, 256), b),
            jax.ShapeDtypeStruct((128, 32 * PADDED), b),
        ],
        in_specs=vmem_specs(3),
        out_specs=vmem_specs(3),
        scratch_shapes=[pltpu.SemaphoreType.DMA((18,))] * 4,
        compiler_params=params(0),
        name="gather_weights",
    )(qkv, out, tokens)
    return full_qkv.reshape(32 * PADDED, 384), full_o.reshape(32 * PADDED, 256), normed_pad


def f32(v):
    return v.astype(jnp.float32)


def bf(v):
    return v.astype(jnp.bfloat16)


def copier(send, recv):
    def copy(n, src, dst, to):
        cp = pltpu.make_async_remote_copy(
            src_ref=src, dst_ref=dst, send_sem=send.at[n], recv_sem=recv.at[n],
            device_id=to, device_id_type=MESH,
        )
        cp.start()
        return cp

    return copy


def take_turns(*parts):
    running = list(parts)
    while running:
        for part in list(running):
            try:
                next(part)
            except StopIteration:
                running.remove(part)


def scatter_steps(t_ref, out_ref, far, near, stage, acc1, far2, near2, stage2, acc2, last, send, recv):
    c, z, y, x = place()
    e = lax.axis_index(EXP)
    copy = copier(send, recv)

    def dev(zz, yy, xx):
        return (zz * 16 + ((yy + 4) % 4) * 4 + (xx + 4) % 4, e)

    rows = (pl.ds(0, 48), pl.ds(48, 48))
    copies = []

    def ring(along_x):
        me = x if along_x else y
        up = dev(z, y, x + 1) if along_x else dev(z, y + 1, x)
        down = dev(z, y, x - 1) if along_x else dev(z, y - 1, x)
        return me, (me + 3) % 4, (me + 1) % 4, (me + 2) % 4, up, down

    def first_source(h, zsel, pos):
        return t_ref.at[zsel, pos, :, rows[h]] if h == 0 else t_ref.at[zsel, :, pos, rows[h]]

    def second_source(h, zsel, pos):
        return acc1.at[h, zsel, pos]

    final = []
    for phase, source, far_ref, near_ref, stage_ref, acc in (
        (1, first_source, far, near, stage, acc1),
        (2, second_source, far2, near2, stage2, acc2),
    ):
        started = []
        for h in range(2):
            me, low, high, across, up, down = ring((h == 1) == (phase == 1))
            n = (phase - 1) * 12 + h * 6
            started.append([
                copy(n, source(h, 0, across), far_ref.at[h, 0], up),
                copy(n + 1, source(h, 1, across), far_ref.at[h, 1], down),
                copy(n + 2, source(h, 1, high), near_ref.at[h, 0, 1], up),
                copy(n + 3, source(h, 0, low), near_ref.at[h, 1, 0], down),
            ])
        yield
        for h in range(2):
            me, low, high, across, up, down = ring((h == 1) == (phase == 1))
            n = (phase - 1) * 12 + h * 6
            started[h][0].wait_recv()
            stage_ref[h, 0] = bf(f32(source(h, 0, high)[...]) + f32(far_ref[h, 0]))
            started[h].append(copy(n + 4, stage_ref.at[h, 0], near_ref.at[h, 0, 0], up))
            started[h][1].wait_recv()
            stage_ref[h, 1] = bf(f32(source(h, 1, low)[...]) + f32(far_ref[h, 1]))
            started[h].append(copy(n + 5, stage_ref.at[h, 1], near_ref.at[h, 1, 1], down))
        yield
        for h in range(2):
            me = ring((h == 1) == (phase == 1))[0]
            for i in (2, 3, 4, 5):
                started[h][i].wait_recv()
            for zz in range(2):
                acc[h, zz] = bf(
                    f32(source(h, zz, me)[...]) + f32(near_ref[h, 0, zz]) + f32(near_ref[h, 1, zz])
                )
            copies += started[h]
            if phase == 2:
                final.append(copy(24 + h, acc2.at[h, 1 - z], last.at[h], dev(1 - z, y, x)))
    yield
    for h in range(2):
        final[h].wait_recv()
        out_ref[rows[h], :] = bf(f32(acc2[h, z]) + f32(last[h]))
    for cp in copies + final:
        cp.wait_send()


def scatter_scratch(width):
    b = jnp.bfloat16
    return [
        pltpu.VMEM((2, 2, 4, 48, width), b),
        pltpu.VMEM((2, 2, 2, 4, 48, width), b),
        pltpu.VMEM((2, 2, 4, 48, width), b),
        pltpu.VMEM((2, 2, 4, 48, width), b),
        pltpu.VMEM((2, 2, 48, width), b),
        pltpu.VMEM((2, 2, 2, 48, width), b),
        pltpu.VMEM((2, 2, 48, width), b),
        pltpu.VMEM((2, 2, 48, width), b),
        pltpu.VMEM((2, 48, width), b),
        pltpu.SemaphoreType.DMA((26,)),
        pltpu.SemaphoreType.DMA((26,)),
    ]


def exp_peers():
    c = lax.axis_index(CTX)
    e = lax.axis_index(EXP)
    h, k = e // 2, e % 2
    return (c, e + 1 - 2 * k), (c, ((h + 1) % 4) * 2 + k), (c, ((h + 3) % 4) * 2 + k)


def sum_steps(post, part, out, mate, stage, far, near, send, recv):
    e = lax.axis_index(EXP)
    h, k = e // 2, e % 2
    partner, up, down = exp_peers()
    copy = copier(send, recv)
    lanes = (pl.ds(0, 1408), pl.ds(1408, MODEL - 1408))

    def rows(core, block):
        return pl.ds(pl.multiple_of(core * 64 + block * 16, 16), 16)

    high, low, across = (h + 1) % 4, (h + 3) % 4, (h + 2) % 4
    order = (across, high, low, h)
    pair = [copy(i, part.at[rows(1 - k, b)], mate.at[b], partner) for i, b in enumerate(order)]
    yield
    pair[0].wait_recv()
    stage[across] = bf(f32(part[rows(k, across), :]) + f32(mate[across]))
    copies = [
        copy(4, stage.at[across, :, lanes[0]], far.at[:, lanes[0]], up),
        copy(5, stage.at[across, :, lanes[1]], far.at[:, lanes[1]], down),
    ]
    pair[1].wait_recv()
    stage[high] = bf(f32(part[rows(k, high), :]) + f32(mate[high]))
    copies.append(copy(6, stage.at[high, :, lanes[1]], near.at[0, :, lanes[1]], up))
    pair[2].wait_recv()
    stage[low] = bf(f32(part[rows(k, low), :]) + f32(mate[low]))
    copies.append(copy(7, stage.at[low, :, lanes[0]], near.at[1, :, lanes[0]], down))
    yield
    copies[0].wait_recv()
    stage[high, :, lanes[0]] = bf(f32(stage[high, :, lanes[0]]) + f32(far[:, lanes[0]]))
    copies.append(copy(8, stage.at[high, :, lanes[0]], near.at[0, :, lanes[0]], up))
    copies[1].wait_recv()
    stage[low, :, lanes[1]] = bf(f32(stage[low, :, lanes[1]]) + f32(far[:, lanes[1]]))
    copies.append(copy(9, stage.at[low, :, lanes[1]], near.at[1, :, lanes[1]], down))
    pair[3].wait_recv()
    total = f32(part[rows(k, h), :]) + f32(mate[h])
    yield
    for cp in copies[2:]:
        cp.wait_recv()
    mine = rows(k, h)
    out[mine, :] = post(total + f32(near[0]) + f32(near[1]), mine)
    direct = [copy(10, out.at[mine], out.at[mine], up), copy(11, out.at[mine], out.at[mine], down)]
    passed = [copy(12, out.at[mine], out.at[mine], partner)]
    yield
    theirs = rows(k, low), rows(k, high)
    for i, to in enumerate((up, down)):
        direct[i].wait_recv()
        view = out.at[theirs[i], lanes[i]]
        direct.append(copy(13 + i, view, view, to))
    for i in range(2):
        passed.append(copy(15 + i, out.at[theirs[i]], out.at[theirs[i]], partner))
    yield
    for i in range(2):
        direct[2 + i].wait_recv()
        view = out.at[rows(k, across), lanes[i]]
        passed.append(copy(17 + i, view, view, partner))
    yield
    for cp in passed:
        cp.wait_recv()
    for cp in [*pair, *copies, *direct, *passed]:
        cp.wait_send()


def sum_scratch():
    b = jnp.bfloat16
    return [
        pltpu.VMEM((4, 16, MODEL), b),
        pltpu.VMEM((4, 16, MODEL), b),
        pltpu.VMEM((16, MODEL), b),
        pltpu.VMEM((2, 16, MODEL), b),
        pltpu.SemaphoreType.DMA((20,)),
        pltpu.SemaphoreType.DMA((20,)),
    ]


def ring_ctx():
    c = lax.axis_index(CTX)
    e = lax.axis_index(EXP)
    return ((c + 1) % 32, e), ((c + 31) % 32, e)


def drop_into(ref, values):
    for i in range(32):
        ref[:, SHARD * i : SHARD * (i + 1)] = values[:, PADDED * i : PADDED * i + SHARD]


def attention_kernel(
    normed_pad, full_qkv, full_o, tokens, residual, projected, span, attended, prob_ref, part, rim_send, rim_recv, *scratch
):
    c = lax.axis_index(CTX)
    after, before = ring_ctx()
    greet([*exp_peers(), after, before])
    made = bf(dot(normed_pad[...], full_qkv[...]))
    projected[...] = made
    span[128:, :] = made[:, 256:]
    rim = copier(rim_send, rim_recv)(0, span.at[pl.ds(128, 128)], span.at[pl.ds(0, 128)], after)
    query_pos, key_pos = iota((128, 256), 0), iota((128, 256), 1)
    valid = (key_pos <= query_pos + 128) & (key_pos > query_pos) & (key_pos + c * 128 >= 128)
    rim.wait_recv()
    keys, values = span[:, :HEAD_SIZE], span[:, HEAD_SIZE:]
    for h in range(GROUP):
        scores = dot_nt(made[:, HEAD_SIZE * h : HEAD_SIZE * (h + 1)], keys) * 0.125
        weights = jnp.where(valid, jnp.exp(scores), 0.0)
        prob = weights / jnp.sum(weights, axis=-1, keepdims=True)
        prob_ref[h] = prob
        attended[:, HEAD_SIZE * h : HEAD_SIZE * (h + 1)] = bf(dot(bf(prob), values))
    drop_into(part, bf(dot_nt(attended[...], full_o[...])))
    rim.wait_send()
    take_turns(sum_steps(lambda t, m: add_base(t, m, tokens), part, residual, *scratch))


def attention(normed_pad, full_qkv, full_o, tokens):
    b = jnp.bfloat16
    shape = jax.ShapeDtypeStruct
    return pl.pallas_call(
        attention_kernel,
        out_shape=[
            shape((128, MODEL), b), shape((128, 384), b), shape((256, 128), b), shape((128, 256), b),
            shape((4, 128, 256), jnp.float32),
        ],
        in_specs=vmem_specs(4),
        out_specs=vmem_specs(5),
        scratch_shapes=[
            pltpu.VMEM((128, MODEL), b), pltpu.SemaphoreType.DMA((1,)), pltpu.SemaphoreType.DMA((1,)),
        ] + sum_scratch(),
        compiler_params=params(1),
        name="attention",
    )(normed_pad, full_qkv, full_o, tokens)


def last_kernel(
    grad_in_part, moe_part, cotangent, residual, tokens, normed_pad, full_qkv, full_o, projected, span, attended, prob_ref,
    block_out, grad_tokens, sum_qkv, sum_o,
    grad_resid_bf, grad_resid, resid_pad, qkv_grad, rim_out, rim_in, grad_part, terms_qkv, terms_o,
    rim_send, rim_recv, *scratch
):
    after, before = ring_ctx()
    greet([*near_peers(), *exp_peers(), after, before])
    take_turns(
        sum_steps(
            lambda t, m: finish_resid(t, m, cotangent, residual, grad_resid), grad_in_part, grad_resid_bf, *scratch[:6]
        ),
        sum_steps(lambda t, m: add_base(t, m, residual), moe_part, block_out, *scratch[6:12]),
    )

    def term(left, right, terms):
        def four(i, t):
            rows = left[:, pl.ds(pl.multiple_of(i * 384, 128), 384)]
            terms[i // 4, i % 4] = bf(dot_tn(rows, right)).reshape(4, PADDED, right.shape[1])
            return t

        lax.fori_loop(0, 8, four, 0)

    pad_into(resid_pad, grad_resid_bf[...])
    term(resid_pad, attended[...], terms_o)
    output_sum = scatter_steps(terms_o, sum_o, *scratch[18:29])
    next(output_sum)

    attended_grad = bf(dot(resid_pad[...], full_o[...]))
    keys, values = span[:, :HEAD_SIZE], span[:, HEAD_SIZE:]
    grad_key = jnp.zeros((256, HEAD_SIZE), jnp.float32)
    grad_value = jnp.zeros((256, HEAD_SIZE), jnp.float32)
    for h in range(GROUP):
        head = pl.ds(HEAD_SIZE * h, HEAD_SIZE)
        grad_out = attended_grad[:, HEAD_SIZE * h : HEAD_SIZE * (h + 1)]
        prob = prob_ref[h]
        grad_prob = dot_nt(grad_out, values)
        grad_value = grad_value + dot_tn(bf(prob), grad_out)
        inner = jnp.sum(grad_prob * prob, axis=-1, keepdims=True)
        grad_score = bf(prob * (grad_prob - inner) * 0.125)
        qkv_grad[:, head] = bf(dot(grad_score, keys))
        grad_key = grad_key + dot_tn(grad_score, projected[:, head])
    rim_out[:, :HEAD_SIZE] = bf(grad_key[:128])
    rim_out[:, HEAD_SIZE:] = bf(grad_value[:128])
    rim = copier(rim_send, rim_recv)(0, rim_out, rim_in, before)

    next(output_sum)
    rim.wait()
    qkv_grad[:, 256:320] = bf(grad_key[128:] + f32(rim_in[:, :HEAD_SIZE]))
    qkv_grad[:, 320:] = bf(grad_value[128:] + f32(rim_in[:, HEAD_SIZE:]))
    grads = qkv_grad[...]
    drop_into(grad_part, bf(dot_nt(grads, full_qkv[...])))
    token_sum = sum_steps(
        lambda t, m: finish_tokens(t, m, tokens, grad_resid), grad_part, grad_tokens, *scratch[12:18]
    )
    next(token_sum)
    term(normed_pad, grads, terms_qkv)
    take_turns(scatter_steps(terms_qkv, sum_qkv, *scratch[29:]), output_sum, token_sum)


def last_sums(*operands):
    b = jnp.bfloat16
    shape = jax.ShapeDtypeStruct
    return pl.pallas_call(
        last_kernel,
        out_shape=[shape((128, MODEL), b), shape((128, MODEL), b), shape((PADDED, 384), b), shape((PADDED, 256), b)],
        in_specs=vmem_specs(12),
        out_specs=vmem_specs(4),
        scratch_shapes=[
            pltpu.VMEM((128, MODEL), b),
            pltpu.VMEM((16, MODEL), jnp.float32),
            pltpu.VMEM((128, 32 * PADDED), b),
            pltpu.VMEM((128, 384), b),
            pltpu.VMEM((128, 128), b),
            pltpu.VMEM((128, 128), b),
            pltpu.VMEM((128, MODEL), b),
            pltpu.VMEM((2, 4, 4, PADDED, 384), b),
            pltpu.VMEM((2, 4, 4, PADDED, 256), b),
            pltpu.SemaphoreType.DMA((1,)),
            pltpu.SemaphoreType.DMA((1,)),
        ] + sum_scratch() * 3 + scatter_scratch(256) + scatter_scratch(384),
        compiler_params=params(4),
        name="last_sums",
    )(*operands)


EPSILON = 1e-05
GLU_ALPHA = 1.702
QUERY_HEADS = 32
KEY_VALUE_HEADS = 8
HEAD_SIZE = 64
WINDOW = 128
MODEL = 2880
GROUP = QUERY_HEADS // KEY_VALUE_HEADS


def dot(a, b):
    return jnp.dot(a, b, preferred_element_type=jnp.float32)


def dot_tn(a, b):
    return lax.dot_general(a, b, (((0,), (0,)), ((), ())), preferred_element_type=jnp.float32)


def dot_nt(a, b):
    return lax.dot_general(a, b, (((1,), (1,)), ((), ())), preferred_element_type=jnp.float32)


def inverse_rms(values):
    return lax.rsqrt(jnp.mean(values * values, axis=-1, keepdims=True) + EPSILON)


def rms_back(values, inv_rms, grad_in):
    inner_mean = jnp.mean(grad_in * values, axis=-1, keepdims=True)
    return inv_rms * grad_in - values * (inv_rms * inv_rms * inv_rms) * inner_mean


def iota(shape, axis):
    return lax.broadcasted_iota(jnp.int32, shape, axis)


def spread_extra(q):
    r, j = iota((128, 512), 0), iota((128, 512), 1)
    return bf((j == (r // 4) * 16 + q * 4 + r % 4).astype(jnp.float32))


def expert_kernel(
    x_ref, cot_ref, ids_ref, combine_ref, wg, wu, wd,
    grad_in_part, moe_part, grad_gate, grad_up, grad_down,
    xp, one_hot, extra_hot, weight_ref, scale, send_buf, got, ext, gate_pre, up_pre, act, gg, gu, parts, other, back,
    send, recv, send2, recv2, send3, recv3, send4, recv4,
):
    c = lax.axis_index(CTX)
    e = lax.axis_index(EXP)
    k = e % 2
    partner = (c, e + 1 - 2 * k)
    group, inner = c // 8, c % 8
    barrier = pltpu.get_barrier_semaphore()

    def moved(n, sign):
        return ((group + sign * (n // 8) + 4) % 4) * 8 + (inner + sign * (n % 8) + 8) % 8

    def hello(n, t):
        pl.semaphore_signal(barrier, inc=1, device_id=(moved(n, 1), e), device_id_type=MESH)
        return t

    lax.fori_loop(1, 32, hello, 0)
    pl.semaphore_signal(barrier, inc=1, device_id=partner, device_id_type=MESH)

    lane = iota((128, 512), 1)
    hot = jnp.zeros((128, 512), jnp.float32)
    weight = jnp.zeros((128, 512), jnp.float32)
    for route in range(4):
        match = ids_ref[:, route : route + 1] == lane // 16
        hot = jnp.where(match, 1.0, hot)
        weight = jnp.where(match, combine_ref[:, route : route + 1], weight)
    weight_ref[...] = weight
    below = bf(jnp.where(iota((128, 128), 0) > iota((128, 128), 1), 1.0, 0.0))
    slot = jnp.where(hot > 0, dot(below, bf(hot)), 64.0)
    main = slot == f32(lane % 16)
    extra = slot == f32(16 + lane % 4)
    one_hot[...] = bf(jnp.where(main, 1.0, 0.0))
    for q in range(4):
        extra_hot[q] = bf(jnp.where(extra & (lane % 16 // 4 == q), 1.0, 0.0))
    scale[0] = jnp.sum(jnp.where(main, weight, 0.0).T, axis=1, keepdims=True)
    scale[1] = jnp.sum(jnp.where(extra, weight, 0.0).T, axis=1, keepdims=True)
    res = f32(x_ref[...])
    for a, rows in enumerate((bf(res * inverse_rms(res)), cot_ref[...])):
        xp[a, :, :MODEL] = rows
        xp[a, :, MODEL:] = jnp.zeros((128, 192), jnp.bfloat16)

    def out_copy(a, n):
        to = moved(n, 1)
        return pltpu.make_async_remote_copy(
            src_ref=send_buf.at[a, to], dst_ref=got.at[a, k, c],
            send_sem=send.at[a, n], recv_sem=recv.at[a, n],
            device_id=(to, e), device_id_type=MESH,
        )

    def over(a, n):
        source = moved(n, -1)
        return pltpu.make_async_remote_copy(
            src_ref=got.at[a, k, source], dst_ref=got.at[a, k, source],
            send_sem=send2.at[a, n], recv_sem=recv2.at[a, n],
            device_id=partner, device_id_type=MESH,
        )

    def pack(a, j, t):
        g = (group + j) % 4
        at = pl.ds(pl.multiple_of(g * 128, 128), 128)
        dest = pl.ds(g * 8, 8)
        m = one_hot[:, at]
        s0 = scale[0, at, :] if a else 1.0
        s1 = scale[1, at, :] if a else 1.0

        @pl.when(k == 0)
        def _():
            low = dot_tn(m, xp[a, :, :HALF_LANES])
            send_buf[a, dest] = bf(low * s0 if a else low).reshape(8, 16, HALF_LANES)

        @pl.when(k == 1)
        def _():
            high = dot_tn(m, xp[a, :, HALF_LANES:2944])
            send_buf[a, dest, :, 0:1024] = bf(high * s0 if a else high).reshape(8, 16, 1024)
            quarters = dot_tn(extra_hot[0, :, at], xp[a, :, 0:768])
            for q in range(1, 4):
                quarters = quarters + dot_tn(extra_hot[q, :, at], xp[a, :, 768 * q : 768 * q + 768])
            send_buf[a, dest, :, 1024:1792] = bf(quarters * s1 if a else quarters).reshape(8, 16, 768)
            send_buf[a, dest, :, 1792:] = jnp.zeros((8, 16, 128), jnp.bfloat16)

        return t

    def start_group(a, j):
        first = 1 if j == 0 else 0
        lax.fori_loop(first, 8, lambda i, t: (out_copy(a, j * 8 + i).start(), t)[1], 0)

    for a in range(2):
        for j in range(4):
            pack(a, j, 0)
            if a == 0 and j == 0:
                pl.semaphore_wait(barrier, 32)
            start_group(a, j)
        got[a, k, c] = send_buf[a, c]
        over(a, 0).start()

    def arrived(a, n, t):
        out_copy(a, n).wait_recv()
        over(a, n).start()
        return t

    def take(a):
        lax.fori_loop(1, 32, lambda n, t: arrived(a, n, t), 0)
        lax.fori_loop(0, 32, lambda n, t: (over(a, n).wait(), t)[1], 0)
        packed = got[a, 1, :, :, 1024:1792].reshape(512, 768)
        for q in range(4):
            ext[a, :, 768 * q : 768 * q + 768] = bf(dot(spread_extra(q), packed))

    def rows_of(a, t):
        first = got[a, 0, pl.ds(t * 16, 16)].reshape(256, HALF_LANES)
        second = got[a, 1, pl.ds(t * 16, 16), :, 0:960].reshape(256, 960)
        return first, second

    def at_rows(t):
        return pl.ds(pl.multiple_of(t * 256, 256), 256)

    take(0)

    def forward(t, carry):
        first, second = rows_of(0, t)
        for w, into in ((wg, gate_pre), (wu, up_pre)):
            into[at_rows(t), :] = dot(first, w[:HALF_LANES]) + dot(second, w[HALF_LANES:])
        return carry

    lax.fori_loop(0, 2, forward, 0)
    for w, into in ((wg, gate_pre), (wu, up_pre)):
        into[512:, :] = dot(ext[0, :, :MODEL], w[...])

    take(1)

    def pointwise(rows, grad_act):
        gate, up = gate_pre[rows, :], up_pre[rows, :] + 1.0
        sig = jax.nn.sigmoid(GLU_ALPHA * gate)
        glu = gate * sig
        act[rows, :] = bf(glu * up)
        gg[rows, :] = bf(grad_act * up * (sig + GLU_ALPHA * glu * (1.0 - sig)))
        gu[rows, :] = bf(grad_act * glu)

    def backward(t, carry):
        first, second = rows_of(1, t)
        pointwise(at_rows(t), dot_nt(first, wd[:, :HALF_LANES]) + dot_nt(second, wd[:, HALF_LANES:]))
        return carry

    lax.fori_loop(0, 2, backward, 0)
    pointwise(pl.ds(512, 128), dot_nt(ext[1, :, :MODEL], wd[...]))

    for a in range(2):
        lax.fori_loop(1, 32, lambda n, t, a=a: (out_copy(a, n).wait_send(), t)[1], 0)

    def across(a, j):
        block = pl.ds(((group + j) % 4) * 8, 8)
        return pltpu.make_async_remote_copy(
            src_ref=parts.at[a, 1 - k, block], dst_ref=other.at[a, block],
            send_sem=send3.at[a, j], recv_sem=recv3.at[a, j],
            device_id=partner, device_id_type=MESH,
        )

    def home(a, n):
        to = moved(n, 1)
        return pltpu.make_async_remote_copy(
            src_ref=send_buf.at[a, to], dst_ref=back.at[a, c],
            send_sem=send4.at[a, n], recv_sem=recv4.at[a, n],
            device_id=(to, e), device_id_type=MESH,
        )

    def result(a, rows):
        if a == 0:
            return bf(dot_nt(gg[rows, :], wg[...]) + dot_nt(gu[rows, :], wu[...]))
        return bf(dot(act[rows, :], wd[...]))

    def add_pair(a, j):
        across(a, j).wait_recv()

        def one(i, t):
            n = j * 8 + i
            to = moved(n, 1)
            send_buf[a, to] = bf(f32(parts[a, k, to]) + f32(other[a, to]))

            @pl.when(n > 0)
            def _():
                home(a, n).start()

            return t

        lax.fori_loop(0, 8, one, 0)
        if j == 0:
            back[a, c] = send_buf[a, c]

    steps = [(a, j) for a in range(2) for j in range(4)]
    for index, (a, j) in enumerate(steps):
        if j == 0:
            last = result(a, pl.ds(512, 128))
            folded = jnp.zeros((512, 768), jnp.float32)
            for q in range(4):
                width = 768 if q < 3 else 576
                piece = dot_tn(spread_extra(q), last[:, 768 * q : 768 * q + width])
                if q == 3:
                    piece = jnp.concatenate([piece, jnp.zeros((512, 192), jnp.float32)], axis=1)
                folded = folded + piece
            parts[a, 1, :, :, 1024:1792] = bf(folded).reshape(32, 16, 768)
            parts[a, 1, :, :, 960:1024] = jnp.zeros((32, 16, 64), jnp.bfloat16)
            parts[a, 1, :, :, 1792:] = jnp.zeros((32, 16, 128), jnp.bfloat16)
        g = (group + j) % 4
        rows = result(a, pl.ds(pl.multiple_of(g * 128, 128), 128))
        parts[a, 0, pl.ds(g * 8, 8)] = rows[:, :HALF_LANES].reshape(8, 16, HALF_LANES)
        parts[a, 1, pl.ds(g * 8, 8), :, 0:960] = rows[:, HALF_LANES:].reshape(8, 16, 960)
        across(a, j).start()
        if index:
            add_pair(*steps[index - 1])
    add_pair(*steps[-1])

    def grads_at(columns, lanes, half):
        x_main = got[0, half, :, :, lanes].reshape(512, lanes.size)
        g_main = got[1, half, :, :, lanes].reshape(512, lanes.size)
        x_ext, g_ext = ext[0, :, columns], ext[1, :, columns]
        grad_gate[columns, :] = bf(dot_tn(x_main, gg[:512, :]) + dot_tn(x_ext, gg[512:, :]))
        grad_up[columns, :] = bf(dot_tn(x_main, gu[:512, :]) + dot_tn(x_ext, gu[512:, :]))
        grad_down[:, columns] = bf(dot_tn(act[:512, :], g_main) + dot_tn(act[512:, :], g_ext))

    def lower(i, t):
        lanes = pl.ds(pl.multiple_of(i * 384, 128), 384)
        grads_at(lanes, lanes, 0)
        return t

    lax.fori_loop(0, 5, lower, 0)
    grads_at(pl.ds(1920, 512), pl.ds(0, 512), 1)
    grads_at(pl.ds(2432, 448), pl.ds(512, 448), 1)

    for a, into in enumerate((grad_in_part, moe_part)):
        lax.fori_loop(1, 32, lambda n, t, a=a: (home(a, n).wait_recv(), t)[1], 0)

        def summed(hot, lanes, a=a):
            rows = back[a, :, :, lanes].reshape(512, lanes.size)
            if a == 0:
                return dot(hot, rows)
            spread = jnp.where(hot > 0, weight_ref[...], 0.0)
            high = bf(spread)
            return dot(high, rows) + dot(bf(spread - f32(high)), rows)

        @pl.when(k == 0)
        def _(into=into, summed=summed):
            into[:, :HALF_LANES] = bf(summed(one_hot[...], pl.ds(0, HALF_LANES)))
            into[:, HALF_LANES:] = jnp.zeros((128, 960), jnp.bfloat16)

        @pl.when(k == 1)
        def _(into=into, summed=summed):
            upper = summed(one_hot[...], pl.ds(0, 1024))
            quarters = [summed(extra_hot[q], pl.ds(1024, 768)) for q in range(4)]
            into[:, 0:768] = bf(quarters[0])
            into[:, 768:1536] = bf(quarters[1])
            into[:, 1536:1920] = bf(quarters[2][:, :384])
            into[:, 1920:2304] = bf(quarters[2][:, 384:] + upper[:, :384])
            into[:, 2304:] = bf(quarters[3][:, :576] + upper[:, 384:960])

    for a in range(2):
        lax.fori_loop(1, 32, lambda n, t, a=a: (home(a, n).wait_send(), t)[1], 0)
        lax.fori_loop(0, 4, lambda j, t, a=a: (across(a, j).wait_send(), t)[1], 0)


def experts(residual, cotangent, expert_ids, combine_weights, w_gate, w_up, w_down):
    b = jnp.bfloat16
    shape = jax.ShapeDtypeStruct
    return pl.pallas_call(
        expert_kernel,
        out_shape=[
            shape((128, MODEL), b), shape((128, MODEL), b),
            shape((MODEL, 256), b), shape((MODEL, 256), b), shape((256, MODEL), b),
        ],
        in_specs=vmem_specs(7),
        out_specs=vmem_specs(5),
        scratch_shapes=[
            pltpu.VMEM((2, 128, 3072), b),
            pltpu.VMEM((128, 512), b),
            pltpu.VMEM((4, 128, 512), b),
            pltpu.VMEM((128, 512), jnp.float32),
            pltpu.VMEM((2, 512, 1), jnp.float32),
            pltpu.VMEM((2, 32, 16, HALF_LANES), b),
            pltpu.VMEM((2, 2, 32, 16, HALF_LANES), b),
            pltpu.VMEM((2, 128, 3072), b),
            pltpu.VMEM((640, 256), jnp.float32),
            pltpu.VMEM((640, 256), jnp.float32),
            pltpu.VMEM((640, 256), b),
            pltpu.VMEM((640, 256), b),
            pltpu.VMEM((640, 256), b),
            pltpu.VMEM((2, 2, 32, 16, HALF_LANES), b),
            pltpu.VMEM((2, 32, 16, HALF_LANES), b),
            pltpu.VMEM((2, 32, 16, HALF_LANES), b),
        ] + [pltpu.SemaphoreType.DMA((2, 32))] * 4
        + [pltpu.SemaphoreType.DMA((2, 4))] * 2 + [pltpu.SemaphoreType.DMA((2, 32))] * 2,
        compiler_params=params(2),
        name="experts",
    )(residual, cotangent, expert_ids, combine_weights, w_gate, w_up, w_down)


def add_base(total, mine, base):
    return bf(f32(base[mine, :]) + total)


def finish_resid(total, mine, cot, resid, grad_resid):
    values = f32(resid[mine, :])
    out = f32(cot[mine, :]) + rms_back(values, inverse_rms(values), total)
    grad_resid[...] = out
    return bf(out)


def finish_tokens(total, mine, tokens, grad_resid):
    values = f32(tokens[mine, :])
    return bf(grad_resid[...] + rms_back(values, inverse_rms(values), total))


def body(
    tokens, cotangent, expert_ids, combine_weights,
    w_query, key_value_weight, w_output, w_gate, w_up, w_down,
):
    widen = lambda v: jnp.pad(v, ((0, PADDED - SHARD), (0, 0)))
    full_qkv, full_o, normed_pad = gather_weights(
        widen(jnp.concatenate([w_query, key_value_weight], axis=1)), widen(w_output.T), tokens
    )
    residual, projected, span, attended, prob = attention(normed_pad, full_qkv, full_o, tokens)
    grad_in_part, moe_part, grad_gate, grad_up, grad_down = experts(
        residual, cotangent, expert_ids, combine_weights, w_gate[0], w_up[0], w_down[0]
    )
    block_out, grad_tokens, sum_qkv, sum_o = last_sums(
        grad_in_part, moe_part, cotangent, residual, tokens, normed_pad, full_qkv, full_o, projected, span, attended, prob
    )
    return (
        block_out, grad_tokens, sum_qkv[:SHARD, :256], sum_qkv[:SHARD, 256:], sum_o[:SHARD].T,
        grad_gate[None], grad_up[None], grad_down[None],
    )


def solution(mesh):
    in_specs = (
        P("ctx", None), P("ctx", None), P("ctx", None), P("ctx", None),
        P("ctx", "exp"), P("ctx", "exp"), P("exp", "ctx"),
        P("ctx", None, "exp"), P("ctx", None, "exp"), P("ctx", "exp", None),
    )
    out_specs = (
        P("ctx", None), P("ctx", None), P("ctx", "exp"), P("ctx", "exp"), P("exp", "ctx"),
        P("ctx", None, "exp"), P("ctx", None, "exp"), P("ctx", "exp", None),
    )
    return jax.shard_map(body, mesh=mesh, in_specs=in_specs, out_specs=out_specs, check_vma=False)
```
